512 devices in a mesh: prompt: 16 (over x, y_hi, core), branch: 32 (over z, y_lo).
Axes of the slice: x: 4, y: 4 (y_hi: 2, y_lo: 2; y = y_hi * 2 + y_lo), z: 16, core: 2. Of those that a mesh axis runs over, the one named last changes fastest.
Arguments:
- queries: bfloat16 [16, 32, 256, 1024], P('prompt', 'branch'), may hold values from -8 to 8
- resp_keys: bfloat16 [16, 32, 256, 128], P('prompt', 'branch'), may hold values from -6 to 6
- resp_values: bfloat16 [16, 32, 256, 128], P('prompt', 'branch'), may hold values from -6 to 6
- trunk_keys: bfloat16 [16, 1024, 128], P('prompt', 'branch'), may hold values from -8 to 8
- trunk_values: bfloat16 [16, 1024, 128], P('prompt', 'branch'), may hold values from -6 to 6
- header_keys: bfloat16 [512, 128], P('prompt'), may hold values from -6 to 6
- header_values: bfloat16 [512, 128], P('prompt'), may hold values from -6 to 6
- out_grad: bfloat16 [16, 32, 256, 1024], P('prompt', 'branch'), may hold values from -96 to 96
- lengths: int32 [16, 32], P('prompt', 'branch'), may hold values from 64 to 256, as said below
- forks: int32 [16, 32], P('prompt', 'branch'), may hold values from 1 to 8, as said below
Outputs:
- query_grad: bfloat16 [16, 32, 256, 1024], P('prompt', 'branch')
- resp_key_grad: bfloat16 [16, 32, 256, 128], P('prompt', 'branch')
- resp_value_grad: bfloat16 [16, 32, 256, 128], P('prompt', 'branch')
- trunk_key_grad: float32 [16, 1024, 128], P('prompt', 'branch')
- trunk_value_grad: float32 [16, 1024, 128], P('prompt', 'branch')
- header_key_grad: float32 [512, 128], P('prompt')
- header_value_grad: float32 [512, 128], P('prompt')
The draws below stay inside these ranges and needn't reach their ends.
Inputs may be any that keep to these rules, and one draw needn't show every extreme that they name: `lengths`: every prompt has one response of exactly 256 live tokens. `forks`: every prompt has one response that sees all 8 trunk blocks.
All inputs are finite; a program needn't handle non-finite values.
Results may differ from the reference program's by a relative error of at most 0.0087.
Values may be sent and summed in bfloat16 or wider, within the bound.
A program may use at most 64 MiB of HBM per device.

```python
import jax
import jax.numpy as jnp
from jax import lax

DH = 128
H = 8
BLK = 128
RESP = 256
PROMPTS = 16
BRANCHES = 32
PREF = 1024
HDR = 512
NTB = 8


def draw_queries(key, part):
    key = jax.random.fold_in(key, 11)
    shape = (PROMPTS, BRANCHES, RESP, H * DH)
    return jnp.clip(jax.random.normal(key, shape, jnp.float32), -6.0, 6.0).astype(jnp.bfloat16)


def draw_trunk_keys(key, part):
    key = jax.random.fold_in(key, 12)
    shape = (PROMPTS, PREF, DH)
    return jnp.clip(jax.random.normal(key, shape, jnp.float32), -6.0, 6.0).astype(jnp.bfloat16)


def draw_lengths(key, part):
    key = jax.random.fold_in(key, 21)
    len_key, pick_key = jax.random.split(key)
    drawn_len = jax.random.randint(len_key, (PROMPTS, BRANCHES), RESP // 4, RESP + 1)
    picked = jax.random.randint(pick_key, (PROMPTS, 1), 0, BRANCHES)
    branch_ids = jnp.arange(BRANCHES)[None, :]
    return jnp.where(branch_ids == picked, RESP, drawn_len).astype(jnp.int32)


def draw_forks(key, part):
    key = jax.random.fold_in(key, 31)
    fork_key, pick_key = jax.random.split(key)
    drawn_fork = jax.random.randint(fork_key, (PROMPTS, BRANCHES), 1, NTB + 1)
    picked = jax.random.randint(pick_key, (PROMPTS, 1), 0, BRANCHES)
    branch_ids = jnp.arange(BRANCHES)[None, :]
    return jnp.where(branch_ids == picked, NTB, drawn_fork).astype(jnp.int32)


def levels(own_key, dims, pieces, least, high):
    def one(axis_at, blocks):
        draws = jax.random.uniform(jax.random.fold_in(jax.random.fold_in(own_key, 6), axis_at), (blocks,), jnp.float32, least / len(pieces), high / len(pieces))
        return jnp.repeat(jnp.exp(draws), dims[axis_at] // blocks).reshape((-1,) + (1,) * (len(dims) - axis_at - 1))

    loudness = one(*pieces[0])
    for cut in pieces[1:]:
        loudness = loudness * one(*cut)
    return loudness


def gaussian(own_key, dims, width, most, cuts=(), kind=jnp.bfloat16):
    result = jax.random.normal(own_key, dims, jnp.float32) * width
    if len(cuts) > 0:
        result = levels(own_key, dims, cuts, -0.22, 0.18) * result
    return jnp.clip(result, min=-most, max=most).astype(kind)


def setup_inputs(seed: int = 0) -> dict:
    arg_keys = jax.random.split(jax.random.key(seed), 11)
    return {
        "queries": draw_queries(jax.random.fold_in(arg_keys[10], 71), 0),
        "resp_keys": gaussian(arg_keys[1], (PROMPTS, BRANCHES, RESP, DH), 1.0, 6.0, ((0, 16), (1, 32))),
        "resp_values": gaussian(arg_keys[2], (PROMPTS, BRANCHES, RESP, DH), 1.0, 6.0, ((0, 16), (1, 32))),
        "trunk_keys": draw_trunk_keys(jax.random.fold_in(arg_keys[10], 71), 0),
        "trunk_values": gaussian(arg_keys[4], (PROMPTS, PREF, DH), 1.0, 6.0, ((0, 16), (1, 32))),
        "header_keys": gaussian(arg_keys[5], (HDR, DH), 1.0, 6.0, ((0, 16),)),
        "header_values": gaussian(arg_keys[6], (HDR, DH), 1.0, 6.0, ((0, 16),)),
        "out_grad": gaussian(arg_keys[7], (PROMPTS, BRANCHES, RESP, H * DH), 16.0, 96.0, ((0, 16), (1, 32))),
        "lengths": draw_lengths(jax.random.fold_in(arg_keys[10], 71), 0),
        "forks": draw_forks(jax.random.fold_in(arg_keys[10], 71), 0),
    }


MASKED_SCORE = -1e30


def response_grads(query_rows, resp_k, resp_v, dout, length, fork_depth, trunk_k, trunk_v, head_k, head_v):
    row_count = RESP * H
    score_scale = DH ** -0.5
    query_flat = query_rows.reshape(row_count, DH)
    live_rows = jnp.arange(RESP) < length
    grad_flat = jnp.where(live_rows[:, None], dout, jnp.zeros_like(dout)).reshape(row_count, DH)
    all_keys = jnp.concatenate([head_k, trunk_k, resp_k], axis=0)
    all_values = jnp.concatenate([head_v, trunk_v, resp_v], axis=0)
    column = jnp.arange(HDR + PREF + RESP)[None, :]
    query_pos = (jnp.arange(row_count) // H)[:, None]
    in_head = column < HDR
    in_trunk = (column >= HDR) & (column < HDR + PREF) & ((column - HDR) // BLK < fork_depth)
    in_resp = (column >= HDR + PREF) & (column - HDR - PREF <= query_pos)
    raw = jnp.dot(query_flat, all_keys.T, preferred_element_type=jnp.float32) * score_scale
    logits = jnp.where(in_head | in_trunk | in_resp, raw, MASKED_SCORE)
    row_max = jnp.max(logits, axis=1, keepdims=True)
    log_total = row_max + jnp.log(jnp.sum(jnp.exp(logits - row_max), axis=1, keepdims=True))
    prob_full = jnp.exp(logits - log_total)
    prob_grad = jnp.dot(grad_flat, all_values.T, preferred_element_type=jnp.float32)
    row_delta = jnp.sum(prob_full * prob_grad, axis=1, keepdims=True)
    score_grad = (prob_full * (prob_grad - row_delta) * score_scale).astype(jnp.bfloat16)
    prob_low = prob_full.astype(jnp.bfloat16)
    query_grad = jnp.dot(score_grad, all_keys, preferred_element_type=jnp.float32).astype(jnp.bfloat16).reshape(RESP, H * DH)
    key_grad = jnp.dot(score_grad.T, query_flat, preferred_element_type=jnp.float32)
    value_grad = jnp.dot(prob_low.T, grad_flat, preferred_element_type=jnp.float32)
    return query_grad, key_grad, value_grad


def reference(queries, resp_keys, resp_values, trunk_keys, trunk_values, header_keys, header_values, out_grad, lengths, forks):
    def per_prompt(head_sums, prompt_idx):
        trunk_k = trunk_keys[prompt_idx]
        trunk_v = trunk_values[prompt_idx]

        def per_branch(carried, branch_idx):
            query_grad, key_grad, value_grad = response_grads(
                queries[prompt_idx, branch_idx], resp_keys[prompt_idx, branch_idx],
                resp_values[prompt_idx, branch_idx], out_grad[prompt_idx, branch_idx],
                lengths[prompt_idx, branch_idx], forks[prompt_idx, branch_idx],
                trunk_k, trunk_v, header_keys, header_values)
            trunk_ksum, trunk_vsum, head_ksum, head_vsum = carried
            trunk_ksum = trunk_ksum + key_grad[HDR:HDR + PREF]
            trunk_vsum = trunk_vsum + value_grad[HDR:HDR + PREF]
            head_ksum = head_ksum + key_grad[:HDR]
            head_vsum = head_vsum + value_grad[:HDR]
            outputs = (query_grad, key_grad[HDR + PREF:].astype(jnp.bfloat16), value_grad[HDR + PREF:].astype(jnp.bfloat16))
            return (trunk_ksum, trunk_vsum, head_ksum, head_vsum), outputs

        trunk_zero = jnp.zeros((PREF, DH), jnp.float32)
        start_carry = (trunk_zero, trunk_zero, head_sums[0], head_sums[1])
        finals, outputs = lax.scan(per_branch, start_carry, jnp.arange(BRANCHES))
        trunk_ksum, trunk_vsum, head_ksum, head_vsum = finals
        query_grad, resp_kgrad, resp_vgrad = outputs
        return (head_ksum, head_vsum), (query_grad, resp_kgrad, resp_vgrad, trunk_ksum, trunk_vsum)

    head_zero = jnp.zeros((HDR, DH), jnp.float32)
    head_sums, outputs = lax.scan(per_prompt, (head_zero, head_zero), jnp.arange(PROMPTS))
    query_grad, resp_kgrad, resp_vgrad, trunk_kgrad, trunk_vgrad = outputs
    return (query_grad, resp_kgrad, resp_vgrad, trunk_kgrad, trunk_vgrad,
            head_sums[0], head_sums[1])
```

```python
import functools

import jax
import jax.numpy as jnp
from jax import lax
from jax.experimental import pallas as pl
from jax.experimental.pallas import tpu as pltpu
from jax.sharding import PartitionSpec as P

DH = 128
H = 8
BLK = 128
RESP = 256
HDR = 512
PREF = 1024
NP = 16
NB = 32
NZ = 16
CH = 256
KEYS = HDR + PREF + RESP
NCH = KEYS // CH
FAR = 5
NEAR = (-2, -1, 1, 2)
LOW = -1e30
SCALE = DH**-0.5
LOG2E = 1.4426950408889634
C2 = SCALE * LOG2E
MESH = pl.DeviceIdType.MESH
F32 = jnp.float32
BF16 = jnp.bfloat16


def mod(a, n):
    return lax.rem(a + 4 * n, n)


def kernel(
    lengths, forks, q_hbm, rk_hbm, rv_hbm, tk_hbm, tv_hbm, hk_hbm, hv_hbm, g_hbm,
    dq_out, rkg_out, rvg_out, tkg_out, tvg_out, hkg_out, hvg_out,
    qf, gf, qt, gt, ka, va, kt, hkv, tkv, e_s, dp_s, ds_s, m_s, l_s, d_s, mb_s, fac_s, del_s,
    tb, r1, ra, cs, r2, hb, rh, zs, rz, ro, rg,
    in_sem, own_sem, gs, hrs, trs, ars, s1, q1, qa, s2, q2, sh, qh, sz, qz, sg, qg,
):
    p = lax.axis_index("prompt")
    b = lax.axis_index("branch")
    z = b // 2
    y = lax.rem(b, 2)
    yo = 1 - y
    plane = p * 2 + y

    def at(dz, yy):
        return mod(z + dz, NZ) * 2 + yy

    barrier = pltpu.get_barrier_semaphore()
    greet = [(p, at(s * FAR, yy)) for s in (-1, 1) for yy in (y, yo)]
    greet += [(p, at(j, yy)) for j in (-3, -2, -1, 1, 2, 3) for yy in (y, yo)]
    greet += [(p, at(0, yo))]
    greet += [(mod(p + o, NP), b) for o in range(1, NP)]
    for d in greet:
        pl.semaphore_signal(barrier, 1, device_id=d, device_id_type=MESH)

    own = [
        pltpu.make_async_copy(hk_hbm, hkv.at[p, pl.ds(0, 32)], own_sem.at[0]),
        pltpu.make_async_copy(hv_hbm, hkv.at[p, pl.ds(32, 32)], own_sem.at[1]),
        pltpu.make_async_copy(tk_hbm.at[0], tkv.at[b, pl.ds(0, 32)], own_sem.at[2]),
        pltpu.make_async_copy(tv_hbm.at[0], tkv.at[b, pl.ds(32, 32)], own_sem.at[3]),
    ]
    for c in own:
        c.start()
    loads = [
        pltpu.make_async_copy(rk_hbm.at[0, 0], ka.at[pl.ds(HDR + PREF, RESP)], in_sem.at[0]),
        pltpu.make_async_copy(rv_hbm.at[0, 0], va.at[pl.ds(HDR + PREF, RESP)], in_sem.at[1]),
    ]
    for h in range(H):
        loads.append(pltpu.make_async_copy(
            q_hbm.at[0, 0, :, pl.ds(h * DH, DH)], qf.at[pl.ds(h * RESP, RESP)], in_sem.at[2 + h]))
        loads.append(pltpu.make_async_copy(
            g_hbm.at[0, 0, :, pl.ds(h * DH, DH)], gf.at[pl.ds(h * RESP, RESP)], in_sem.at[2 + H + h]))
    for c in loads:
        c.start()

    for c in own:
        c.wait()
    pl.semaphore_wait(barrier, len(greet))

    sent = []

    def send(src, dst, ssem, rsem, dev):
        c = pltpu.make_async_remote_copy(
            src_ref=src, dst_ref=dst, send_sem=ssem, recv_sem=rsem, device_id=dev, device_id_type=MESH)
        c.start()
        sent.append(c)

    n = 0
    slots = [b, at(-FAR, y), at(FAR, y)]
    for s in (-1, 1):
        send(tkv.at[b], tkv.at[b], gs.at[n], trs.at[b], (p, at(s * FAR, y)))
        n += 1
    near = [at(j, yy) for j in NEAR for yy in (y, yo)] + [at(0, yo)]
    for d in near:
        send(tkv.at[b], tkv.at[b], gs.at[n], trs.at[b], (p, d))
        n += 1
    for o in range(1, NP):
        send(hkv.at[p], hkv.at[p], gs.at[n], hrs.at[p], (mod(p + o, NP), b))
        n += 1

    for c in loads:
        c.wait()
    live = lax.broadcasted_iota(jnp.int32, (RESP, DH), 0) < lengths[0, 0]

    def prepare(h, _):
        rows = pl.ds(pl.multiple_of(h * RESP, RESP), RESP)
        g = jnp.where(live, gf[rows, :], jnp.zeros((), BF16))
        gf[rows, :] = g
        gt[h] = g.T
        qt[h] = qf[rows, :].T
        m_s[h] = jnp.full((1, RESP), LOW, F32)
        l_s[h] = jnp.zeros((8, RESP), F32)
        d_s[h] = jnp.zeros((8, RESP), F32)
        return 0

    lax.fori_loop(0, H, prepare, 0)
    fork = forks[0, 0]

    def stats(i, h, kind):
        rows = pl.ds(i * CH if isinstance(i, int) else pl.multiple_of(i * CH, CH), CH)
        s = jnp.dot(ka[rows, :], qt[h], preferred_element_type=F32)
        dp = jnp.dot(va[rows, :], gt[h], preferred_element_type=F32)
        if kind == "resp":
            key = lax.broadcasted_iota(jnp.int32, (CH, RESP), 0)
            pos = lax.broadcasted_iota(jnp.int32, (CH, RESP), 1)
            s = jnp.where(key <= pos, s, LOW)
        m_old = m_s[h]
        halves = []
        m_new = m_old
        for u in range(2):
            top = jnp.max(s[u * BLK : (u + 1) * BLK], axis=0, keepdims=True)
            seen = None
            if kind == "trunk":
                seen = jnp.broadcast_to((i - HDR // CH) * 2 + u, (1, RESP)) < fork
                top = jnp.where(seen, top, LOW)
            halves.append(seen)
            m_new = jnp.maximum(m_new, top)
        f = jnp.exp2((m_old - m_new) * C2)
        shift = m_new * C2
        l = l_s[h] * f
        d = d_s[h] * f
        for u in range(2):
            sh_u = shift if halves[u] is None else jnp.where(halves[u], shift, -LOW)
            e = jnp.exp2(s[u * BLK : (u + 1) * BLK] * C2 - sh_u)
            dpu = dp[u * BLK : (u + 1) * BLK]
            l = l + jnp.sum(e.reshape(BLK // 8, 8, RESP), axis=0)
            d = d + jnp.sum((e * dpu).reshape(BLK // 8, 8, RESP), axis=0)
            r = pl.ds(i * CH + u * BLK if isinstance(i, int) else pl.multiple_of(i * CH + u * BLK, BLK), BLK)
            e_s[h, r, :] = e
            dp_s[h, r, :] = dpu
        l_s[h] = l
        d_s[h] = d
        m_s[h] = m_new
        mb_s[i, h] = m_new

    def stats_of(i, kind):
        def body(h, _):
            stats(i, h, kind)
            return 0
        lax.fori_loop(0, H, body, 0, unroll=2)

    stats_of(NCH - 1, "resp")

    for s in slots[1:]:
        pltpu.make_async_remote_copy(
            src_ref=tkv.at[s], dst_ref=tkv.at[s], send_sem=gs.at[0], recv_sem=trs.at[s],
            device_id=(p, at(1, y)), device_id_type=MESH).wait_recv()
    for s in slots[1:]:
        for d in near:
            send(tkv.at[s], tkv.at[s], gs.at[n], trs.at[s], (p, d))
            n += 1
    kk, vv = pl.ds(0, 32), pl.ds(32, 32)
    for yy in (y, yo):
        send(tkv.at[slots[1], kk], tkv.at[slots[1], kk], gs.at[n], trs.at[slots[1]], (p, at(3, yy)))
        n += 1
        send(tkv.at[slots[2], vv], tkv.at[slots[2], vv], gs.at[n], ars.at[lax.rem(slots[2], 2)], (p, at(-3, yy)))
        n += 1

    def arrived(ref, sem):
        pltpu.make_async_remote_copy(
            src_ref=ref, dst_ref=ref, send_sem=gs.at[0], recv_sem=sem,
            device_id=(p, at(1, y)), device_id_type=MESH).wait_recv()

    for o in range(1, NP):
        s = mod(p + o, NP)
        arrived(hkv.at[s], hrs.at[s])
    for i in range(NP):
        ka[pl.ds(i * 32, 32), :] = hkv[i, :32, :]
        va[pl.ds(i * 32, 32), :] = hkv[i, 32:, :]
    for i in range(HDR // CH):
        stats_of(i, "head")

    for dz in range(-7, 9):
        for yy in (y, yo):
            s = at(dz, yy)
            if dz == 0 and yy is y:
                continue
            if abs(dz) == FAR and yy is y:
                continue
            if dz == 8:
                arrived(tkv.at[s, kk], trs.at[s])
                arrived(tkv.at[s, vv], ars.at[yy])
            else:
                arrived(tkv.at[s], trs.at[s])
    for i in range(NB):
        ka[pl.ds(HDR + i * 32, 32), :] = tkv[i, :32, :]
        va[pl.ds(HDR + i * 32, 32), :] = tkv[i, 32:, :]

    def trunk_stats(i, _):
        stats_of(i, "trunk")
        return 0

    lax.fori_loop(HDR // CH, (HDR + PREF) // CH, trunk_stats, 0)

    def finish(h, _):
        inv = 1.0 / jnp.sum(l_s[h], axis=0, keepdims=True)
        del_s[h] = jnp.sum(d_s[h], axis=0, keepdims=True) * inv
        m = m_s[h]
        for i in range(NCH):
            fac_s[i, h] = jnp.exp2((mb_s[i, h] - m) * C2) * inv
        return 0

    lax.fori_loop(0, H, finish, 0)

    def terms(i):
        rows = pl.ds(i * CH if isinstance(i, int) else pl.multiple_of(i * CH, CH), CH)
        kg = jnp.zeros((CH, DH), F32)
        vg = jnp.zeros((CH, DH), F32)
        for h in range(H):
            pr = e_s[h, rows, :] * fac_s[i, h]
            ds = (pr * (dp_s[h, rows, :] - del_s[h])).astype(BF16)
            ds_s[rows, h * RESP : (h + 1) * RESP] = ds
            kg = kg + jnp.dot(ds, qf[h * RESP : (h + 1) * RESP, :], preferred_element_type=F32)
            vg = vg + jnp.dot(pr.astype(BF16), gf[h * RESP : (h + 1) * RESP, :], preferred_element_type=F32)
        return kg * SCALE, vg

    def head_terms(i, _):
        kg, vg = terms(i)
        kg, vg = kg.astype(BF16), vg.astype(BF16)
        for u in range(CH // 16):
            hb[i * (CH // 16) + u, :16, :] = kg[u * 16 : (u + 1) * 16]
            hb[i * (CH // 16) + u, 16:, :] = vg[u * 16 : (u + 1) * 16]
        return 0

    lax.fori_loop(0, HDR // CH, head_terms, 0)

    n = 0
    for o in range(1, 2 * NP):
        d = mod(plane + o, 2 * NP)
        send(hb.at[d], rh.at[plane], sh.at[n], qh.at[plane], (d // 2, z * 2 + lax.rem(d, 2)))
        n += 1

    def trunk_terms(i, _):
        kg, vg = terms(i)
        kg, vg = kg.astype(BF16), vg.astype(BF16)
        for u in range(CH // 32):
            k = (i - HDR // CH) * (CH // 32) + u
            tb[k, :32, :] = kg[u * 32 : (u + 1) * 32]
            tb[k, 32:, :] = vg[u * 32 : (u + 1) * 32]
        return 0

    lax.fori_loop(HDR // CH, (HDR + PREF) // CH, trunk_terms, 0)

    n = 0
    for jn, j in enumerate(NEAR):
        for f in range(3):
            zd = mod(z + j + (f - 1) * FAR, NZ)
            send(tb.at[pl.ds(2 * zd, 2)], r1.at[jn, f], s1.at[n], q1.at[jn, f], (p, at(j, y)))
            n += 1
    anti = mod(z + 8, NZ)
    send(tb.at[pl.ds(2 * anti, 2), kk], ra.at[0], s1.at[n], qa.at[0], (p, at(3, y)))
    n += 1
    send(tb.at[pl.ds(2 * anti, 2), vv], ra.at[1], s1.at[n], qa.at[1], (p, at(-3, y)))

    kg, vg = terms(NCH - 1)
    rkg_out[0, 0] = kg.astype(BF16)
    rvg_out[0, 0] = vg.astype(BF16)

    for o in range(1, 2 * NP):
        s = mod(plane + o, 2 * NP)
        arrived(rh.at[s], qh.at[s])
    rh[plane] = hb[plane]
    acc = jnp.zeros((32, DH), F32)
    for i in range(2 * NP):
        acc = acc + rh[i].astype(F32)
    for i in range(NZ):
        zs[i, 0:1, :] = acc[i : i + 1]
        zs[i, 1:2, :] = acc[16 + i : 17 + i]
    n = 0
    for o in (8, 7, 9, 6, 10, 5, 11, 4, 12, 3, 13, 2, 14, 1, 15):
        d = mod(z + o, NZ)
        send(zs.at[d], rz.at[z], sz.at[n], qz.at[z], (p, d * 2 + y))
        n += 1

    for jn in range(4):
        for f in range(3):
            arrived(r1.at[jn, f], q1.at[jn, f])
    arrived(ra.at[0], qa.at[0])
    arrived(ra.at[1], qa.at[1])
    n = 0
    for f in (0, 2, 1):
        zd = mod(z + (f - 1) * FAR, NZ)
        total = tb[pl.ds(2 * zd, 2)].astype(F32)
        for jn in range(4):
            total = total + r1[jn, f].astype(F32)
        low, high = total[:, :32], total[:, 32:]
        if f == 2:
            low = low + ra[0].astype(F32)
        if f == 0:
            high = high + ra[1].astype(F32)
        cs[f, :, :32] = low.astype(BF16)
        cs[f, :, 32:] = high.astype(BF16)
        if f != 1:
            for w, yy in enumerate((y, yo)):
                send(cs.at[f, yy], r2.at[f, w], s2.at[n], q2.at[f, w], (p, zd * 2 + yy))
                n += 1
        else:
            send(cs.at[f, yo], r2.at[f, 1], s2.at[n], q2.at[f, 1], (p, at(0, yo)))
            n += 1

    for o in range(1, NZ):
        s = mod(z + o, NZ)
        arrived(rz.at[s], qz.at[s])
    rz[z] = zs[z]
    one = rz[0]
    for i in range(1, NZ):
        one = one + rz[i]
    ro[...] = one
    rg[b] = one
    n = 0
    for o in (16, 15, 17, 14, 18, 13, 19, 12, 20, 11, 21, 10, 22, 9, 23, 8, 24, 7, 25, 6, 26, 5, 27, 4, 28, 3, 29, 2, 30, 1, 31):
        d = mod(b + o, NB)
        send(ro, rg.at[b], sg.at[n], qg.at[b], (p, d))
        n += 1

    kt[...] = ka[...].T

    def query_grad(h, _):
        cols = pl.ds(pl.multiple_of(h * RESP, RESP), RESP)
        acc = jnp.dot(kt[...], ds_s[:, cols], preferred_element_type=F32)
        dq_out[0, 0, :, pl.ds(pl.multiple_of(h * DH, DH), DH)] = (acc * SCALE).T.astype(BF16)
        return 0

    lax.fori_loop(0, H, query_grad, 0)

    for f in range(3):
        for w in range(2):
            if f == 1 and w == 0:
                continue
            arrived(r2.at[f, w], q2.at[f, w])
    total = cs[1, y].astype(F32) + r2[1, 1].astype(F32)
    for f in (0, 2):
        for w in range(2):
            total = total + r2[f, w].astype(F32)
    tkg_out[0] = total[:32]
    tvg_out[0] = total[32:]

    for o in range(1, NB):
        s = mod(b + o, NB)
        arrived(rg.at[s], qg.at[s])
    for i in range(32):
        s = (i % NZ) * 2 + i // NZ
        hkg_out[i : i + 1, :] = rg[s, 0:1, :]
        hvg_out[i : i + 1, :] = rg[s, 1:2, :]
    for c in sent:
        c.wait_send()


def per_device(q, rk, rv, tk, tv, hk, hv, g, lengths, forks):
    vm = pl.BlockSpec(memory_space=pltpu.VMEM)
    hbm = pl.BlockSpec(memory_space=pl.ANY)
    smem = pl.BlockSpec(memory_space=pltpu.SMEM)
    dma = pltpu.SemaphoreType.DMA
    sds = jax.ShapeDtypeStruct
    V = pltpu.VMEM
    return pl.pallas_call(
        kernel,
        out_shape=(
            sds((1, 1, RESP, H * DH), BF16), sds((1, 1, RESP, DH), BF16), sds((1, 1, RESP, DH), BF16),
            sds((1, 32, DH), F32), sds((1, 32, DH), F32), sds((32, DH), F32), sds((32, DH), F32),
        ),
        in_specs=[smem, smem] + [hbm] * 8,
        out_specs=(vm,) * 7,
        scratch_shapes=[
            V((H * RESP, DH), BF16), V((H * RESP, DH), BF16),
            V((H, DH, RESP), BF16), V((H, DH, RESP), BF16),
            V((KEYS, DH), BF16), V((KEYS, DH), BF16), V((DH, KEYS), BF16),
            V((NP, 64, DH), BF16), V((NB, 64, DH), BF16),
            V((H, KEYS, RESP), F32), V((H, KEYS, RESP), F32), V((KEYS, H * RESP), BF16),
            V((H, 1, RESP), F32), V((H, 8, RESP), F32), V((H, 8, RESP), F32),
            V((NCH, H, 1, RESP), F32), V((NCH, H, 1, RESP), F32), V((H, 1, RESP), F32),
            V((NB, 64, DH), BF16), V((4, 3, 2, 64, DH), BF16), V((2, 2, 32, DH), BF16),
            V((3, 2, 64, DH), BF16), V((3, 2, 64, DH), BF16),
            V((2 * NP, 32, DH), BF16), V((2 * NP, 32, DH), BF16),
            V((NZ, 2, DH), F32), V((NZ, 2, DH), F32), V((2, DH), F32), V((NB, 2, DH), F32),
            dma((2 + 2 * H,)), dma((4,)),
            dma((48,)), dma((NP,)), dma((NB,)), dma((2,)),
            dma((14,)), dma((4, 3)), dma((2,)),
            dma((5,)), dma((3, 2)),
            dma((31,)), dma((32,)), dma((15,)), dma((NZ,)), dma((31,)), dma((NB,)),
        ],
        compiler_params=pltpu.CompilerParams(
            collective_id=0, has_side_effects=True, vmem_limit_bytes=52 << 20),
    )(lengths, forks, q, rk, rv, tk, tv, hk, hv, g)


def solution(mesh):
    four, three, two = P("prompt", "branch", None, None), P("prompt", "branch", None), P("prompt", None)
    both = P("prompt", "branch")
    return jax.shard_map(
        per_device,
        mesh=mesh,
        in_specs=(four, four, four, three, three, two, two, four, both, both),
        out_specs=(four, four, four, three, three, two, two),
        check_vma=False,
    )
```

```python
import functools

import jax
import jax.numpy as jnp
from jax import lax
from jax.experimental import pallas as pl
from jax.experimental.pallas import tpu as pltpu
from jax.sharding import PartitionSpec as P

DH = 128
H = 8
BLK = 128
RESP = 256
HDR = 512
PREF = 1024
NP = 16
NB = 32
NZ = 16
CH = 256
KEYS = HDR + PREF + RESP
NCH = KEYS // CH
FAR = 5
NEAR = (-2, -1, 1, 2)
LOW = -1e30
SCALE = DH**-0.5
LOG2E = 1.4426950408889634
C2 = SCALE * LOG2E
UNROLL = 8
MESH = pl.DeviceIdType.MESH
F32 = jnp.float32
BF16 = jnp.bfloat16


def mod(a, n):
    return lax.rem(a + 4 * n, n)


def kernel(
    len_hbm, fork_hbm, q_hbm, rk_hbm, rv_hbm, tk_hbm, tv_hbm, hk_hbm, hv_hbm, g_hbm,
    dq_out, rkg_out, rvg_out, tkg_out, tvg_out, hkg_out, hvg_out,
    qf, gf, qt, gt, ka, va, kt, hkv, tkv, e_s, dp_s, ds_s, m_s, l_s, d_s, mb_s, fac_s, del_s,
    tb, r1, cs, r2, hb, rh, zs, rz, rg,
    lengths, forks, in_sem, own_sem, gs, hrs, trs, ars, s1, q1, s2, q2, sh, qh, sz, qz, sg, qg,
):
    p = lax.axis_index("prompt")
    b = lax.axis_index("branch")
    z = b // 2
    y = lax.rem(b, 2)
    yo = 1 - y
    plane = p * 2 + y

    def at(dz, yy):
        return mod(z + dz, NZ) * 2 + yy

    barrier = pltpu.get_barrier_semaphore()
    greet = [(p, at(s * FAR, yy)) for s in (-1, 1) for yy in (y, yo)]
    greet += [(p, at(j, yy)) for j in (-3, -2, -1, 1, 2, 3) for yy in (y, yo)]
    greet += [(p, at(0, yo))]
    greet += [(mod(p + o, NP), b) for o in range(1, NP)]
    for d in greet:
        pl.semaphore_signal(barrier, 1, device_id=d, device_id_type=MESH)

    own = [
        pltpu.make_async_copy(hk_hbm, hkv.at[p, pl.ds(0, 32)], own_sem.at[0]),
        pltpu.make_async_copy(hv_hbm, hkv.at[p, pl.ds(32, 32)], own_sem.at[1]),
        pltpu.make_async_copy(tk_hbm.at[0], tkv.at[b, pl.ds(0, 32)], own_sem.at[2]),
        pltpu.make_async_copy(tv_hbm.at[0], tkv.at[b, pl.ds(32, 32)], own_sem.at[3]),
    ]
    for c in own:
        c.start()
    loads = [
        pltpu.make_async_copy(rk_hbm.at[0, 0], ka.at[pl.ds(HDR + PREF, RESP)], in_sem.at[0]),
        pltpu.make_async_copy(rv_hbm.at[0, 0], va.at[pl.ds(HDR + PREF, RESP)], in_sem.at[1]),
    ]
    loads.append(pltpu.make_async_copy(len_hbm, lengths, in_sem.at[2 + 2 * H]))
    loads.append(pltpu.make_async_copy(fork_hbm, forks, in_sem.at[3 + 2 * H]))
    for h in range(H):
        loads.append(pltpu.make_async_copy(
            q_hbm.at[0, 0, :, pl.ds(h * DH, DH)], qf.at[pl.ds(h * RESP, RESP)], in_sem.at[2 + h]))
        loads.append(pltpu.make_async_copy(
            g_hbm.at[0, 0, :, pl.ds(h * DH, DH)], gf.at[pl.ds(h * RESP, RESP)], in_sem.at[2 + H + h]))
    for c in loads:
        c.start()

    for c in own:
        c.wait()
    pl.semaphore_wait(barrier, len(greet))

    sent = []

    def send(src, dst, ssem, rsem, dev):
        c = pltpu.make_async_remote_copy(
            src_ref=src, dst_ref=dst, send_sem=ssem, recv_sem=rsem, device_id=dev, device_id_type=MESH)
        c.start()
        sent.append(c)

    n = 0
    slots = [b, at(-FAR, y), at(FAR, y)]
    for s in (-1, 1):
        send(tkv.at[b], tkv.at[b], gs.at[n], trs.at[b], (p, at(s * FAR, y)))
        n += 1
    near = [at(j, yy) for j in NEAR for yy in (y, yo)] + [at(0, yo)]
    for d in near:
        send(tkv.at[b], tkv.at[b], gs.at[n], trs.at[b], (p, d))
        n += 1
    for o in range(1, NP):
        send(hkv.at[p], hkv.at[p], gs.at[n], hrs.at[p], (mod(p + o, NP), b))
        n += 1

    for c in loads:
        c.wait()
    live = lax.broadcasted_iota(jnp.int32, (RESP, DH), 0) < lengths[0, 0]

    def prepare(h, _):
        rows = pl.ds(pl.multiple_of(h * RESP, RESP), RESP)
        g = jnp.where(live, gf[rows, :], jnp.zeros((), BF16))
        gf[rows, :] = g
        gt[h] = g.T
        qt[h] = qf[rows, :].T
        m_s[h] = jnp.full((1, RESP), LOW, F32)
        l_s[h] = jnp.zeros((8, RESP), F32)
        d_s[h] = jnp.zeros((8, RESP), F32)
        return 0

    lax.fori_loop(0, H, prepare, 0)
    r1[4, 0, :, :32, :] = jnp.zeros((2, 32, DH), BF16)
    r1[4, 1] = jnp.zeros((2, 64, DH), BF16)
    r1[4, 2, :, 32:, :] = jnp.zeros((2, 32, DH), BF16)
    fork = forks[0, 0]

    def stats(h, spots, seen, kind):
        keys = [ka[pl.ds(r, c), :] for r, c in spots]
        vals = [va[pl.ds(r, c), :] for r, c in spots]
        keys = keys[0] if len(keys) == 1 else jnp.concatenate(keys, axis=0)
        vals = vals[0] if len(vals) == 1 else jnp.concatenate(vals, axis=0)
        s = jnp.dot(keys, qt[h], preferred_element_type=F32)
        dp = jnp.dot(vals, gt[h], preferred_element_type=F32)
        if kind == "resp":
            key = lax.broadcasted_iota(jnp.int32, s.shape, 0)
            pos = lax.broadcasted_iota(jnp.int32, s.shape, 1)
            s = jnp.where(key <= pos, s, LOW)
        m_old = m_s[h]
        m_new = m_old
        first = 0
        for (r, c), see in zip(spots, seen):
            top = jnp.max(s[first : first + c], axis=0, keepdims=True)
            m_new = jnp.maximum(m_new, top if see is None else jnp.where(see, top, LOW))
            first += c
        f = jnp.exp2((m_old - m_new) * C2)
        shift = m_new * C2
        l = l_s[h] * f
        d = d_s[h] * f
        first = 0
        for (r, c), see in zip(spots, seen):
            move = shift if see is None else jnp.where(see, shift, -LOW)
            e = jnp.exp2(s[first : first + c] * C2 - move)
            dpu = dp[first : first + c]
            l = l + jnp.sum(e.reshape(c // 8, 8, RESP), axis=0)
            d = d + jnp.sum((e * dpu).reshape(c // 8, 8, RESP), axis=0)
            e_s[h, pl.ds(r, c), :] = e
            dp_s[h, pl.ds(r, c), :] = dpu
            first += c
        l_s[h] = l
        d_s[h] = d
        m_s[h] = m_new
        return m_new

    def stats_of(spots, seen, kind, marks):
        def body(h, _):
            m = stats(h, spots, seen, kind)
            for k in marks:
                mb_s[k, h] = m
            return 0
        lax.fori_loop(0, H, body, 0, unroll=UNROLL)

    def trunk_stats(zs_here):
        for zb in zs_here:
            for w in range(2):
                r = pl.ds(pl.multiple_of(HDR + zb * 64 + w * 32, 32), 32)
                ka[r, :] = tkv[2 * zb + w, :32, :]
                va[r, :] = tkv[2 * zb + w, 32:, :]
        spots = [(pl.multiple_of(HDR + zb * 64, 64), 64) for zb in zs_here]
        seen = [jnp.broadcast_to(zb // 2, (1, RESP)) < fork for zb in zs_here]
        stats_of(spots, seen, "trunk", zs_here)

    stats_of([(HDR + PREF, RESP)], [None], "resp", [NZ + 2])

    for s in slots[1:]:
        pltpu.make_async_remote_copy(
            src_ref=tkv.at[s], dst_ref=tkv.at[s], send_sem=gs.at[0], recv_sem=trs.at[s],
            device_id=(p, at(1, y)), device_id_type=MESH).wait_recv()
    for s in slots[1:]:
        for d in near:
            send(tkv.at[s], tkv.at[s], gs.at[n], trs.at[s], (p, d))
            n += 1
    kk, vv = pl.ds(0, 32), pl.ds(32, 32)
    for yy in (y, yo):
        send(tkv.at[slots[1], kk], tkv.at[slots[1], kk], gs.at[n], trs.at[slots[1]], (p, at(3, yy)))
        n += 1
        send(tkv.at[slots[2], vv], tkv.at[slots[2], vv], gs.at[n], ars.at[lax.rem(slots[2], 2)], (p, at(-3, yy)))
        n += 1

    def arrived(ref, sem):
        pltpu.make_async_remote_copy(
            src_ref=ref, dst_ref=ref, send_sem=gs.at[0], recv_sem=sem,
            device_id=(p, at(1, y)), device_id_type=MESH).wait_recv()

    for o in range(1, NP):
        s = mod(p + o, NP)
        arrived(hkv.at[s], hrs.at[s])
    for i in range(NP):
        ka[pl.ds(i * 32, 32), :] = hkv[i, :32, :]
        va[pl.ds(i * 32, 32), :] = hkv[i, 32:, :]

    def head_stats(i, _):
        stats_of([(pl.multiple_of(i * CH, CH), CH)], [None], "head", [NZ + i])
        return 0

    lax.fori_loop(0, HDR // CH, head_stats, 0)

    def group(j):
        return [mod(z + j + f * FAR, NZ) for f in (0, -1, 1)]

    for zb in group(0):
        arrived(tkv.at[2 * zb + yo], trs.at[2 * zb + yo])
    trunk_stats(group(0))

    def near_group(k, _):
        j = ((k + 1) // 2) * (2 * lax.rem(k, 2) - 1)
        for zb in group(j):
            for yy in (y, yo):
                arrived(tkv.at[2 * zb + yy], trs.at[2 * zb + yy])
        trunk_stats(group(j))
        return 0

    lax.fori_loop(1, 5, near_group, 0)
    anti = mod(z + 8, NZ)
    for yy in (y, yo):
        arrived(tkv.at[2 * anti + yy, kk], trs.at[2 * anti + yy])
        arrived(tkv.at[2 * anti + yy, vv], ars.at[yy])
    trunk_stats([anti])

    def finish(h, _):
        inv = 1.0 / jnp.sum(l_s[h], axis=0, keepdims=True)
        del_s[h] = jnp.sum(d_s[h], axis=0, keepdims=True) * inv
        m = m_s[h]
        for i in range(NZ + 3):
            fac_s[i, h] = jnp.exp2((mb_s[i, h] - m) * C2) * inv
        return 0

    lax.fori_loop(0, H, finish, 0)

    def terms(first, marks):
        rows = pl.ds(first, CH)
        c = CH // len(marks)
        kg = jnp.zeros((CH, DH), F32)
        vg = jnp.zeros((CH, DH), F32)
        for h in range(H):
            pr = [e_s[h, pl.ds(first + u * c, c), :] * fac_s[k, h] for u, k in enumerate(marks)]
            pr = pr[0] if len(pr) == 1 else jnp.concatenate(pr, axis=0)
            ds = (pr * (dp_s[h, rows, :] - del_s[h])).astype(BF16)
            ds_s[rows, h * RESP : (h + 1) * RESP] = ds
            kg = kg + jnp.dot(ds, qf[h * RESP : (h + 1) * RESP, :], preferred_element_type=F32)
            vg = vg + jnp.dot(pr.astype(BF16), gf[h * RESP : (h + 1) * RESP, :], preferred_element_type=F32)
        return kg * SCALE, vg

    def head_terms(i, _):
        kg, vg = terms(pl.multiple_of(i * CH, CH), [NZ + i])
        kg, vg = kg.astype(BF16), vg.astype(BF16)
        for u in range(CH // 16):
            hb[i * (CH // 16) + u, :16, :] = kg[u * 16 : (u + 1) * 16]
            hb[i * (CH // 16) + u, 16:, :] = vg[u * 16 : (u + 1) * 16]
        return 0

    lax.fori_loop(0, HDR // CH, head_terms, 0)

    n = 0
    for o in range(1, 2 * NP):
        d = mod(plane + o, 2 * NP)
        send(hb.at[d], rh.at[plane], sh.at[n], qh.at[plane], (d // 2, z * 2 + lax.rem(d, 2)))
        n += 1

    def route(zd):
        o = mod(zd - z, NZ)
        near_it = jnp.logical_or(o <= 2, o >= NZ - 2)
        f = jnp.where(near_it, 1, jnp.where(o <= 8, 2, 0))
        j = jnp.where(o <= 2, o, jnp.where(o <= 8, o - FAR, jnp.where(o <= 13, o - 11, o - NZ)))
        jn = jnp.where(o == 8, 4, jnp.where(j < 0, j + 2, j + 1))
        return o, j, jn, f

    def near_copies(zd):
        o, j, jn, f = route(zd)
        whole = pltpu.make_async_remote_copy(
            src_ref=tb.at[pl.ds(2 * zd, 2)], dst_ref=r1.at[jn, f], send_sem=s1.at[zd], recv_sem=q1.at[jn, f],
            device_id=(p, mod(z + j, NZ) * 2 + y), device_id_type=MESH)
        low = pltpu.make_async_remote_copy(
            src_ref=tb.at[pl.ds(2 * zd, 2), kk], dst_ref=r1.at[4, 2, :, kk], send_sem=s1.at[zd], recv_sem=q1.at[4, 2],
            device_id=(p, at(3, y)), device_id_type=MESH)
        high = pltpu.make_async_remote_copy(
            src_ref=tb.at[pl.ds(2 * zd, 2), vv], dst_ref=r1.at[4, 0, :, vv], send_sem=s1.at[NZ], recv_sem=q1.at[4, 0],
            device_id=(p, at(-3, y)), device_id_type=MESH)
        return jnp.logical_and(o != 8, j != 0), o == 8, whole, low, high

    def trunk_terms(i, _):
        kg, vg = terms(pl.multiple_of(HDR + i * CH, CH), [i * 4 + u for u in range(4)])
        kg, vg = kg.astype(BF16), vg.astype(BF16)
        for u in range(CH // 32):
            k = i * (CH // 32) + u
            tb[k, :32, :] = kg[u * 32 : (u + 1) * 32]
            tb[k, 32:, :] = vg[u * 32 : (u + 1) * 32]
        for u in range(4):
            one, two, whole, low, high = near_copies(i * 4 + u)

            @pl.when(one)
            def _():
                whole.start()

            @pl.when(two)
            def _():
                low.start()
                high.start()
        return 0

    lax.fori_loop(0, PREF // CH, trunk_terms, 0)

    kg, vg = terms(HDR + PREF, [NZ + 2])
    rkg_out[0, 0] = kg.astype(BF16)
    rvg_out[0, 0] = vg.astype(BF16)

    for o in range(1, 2 * NP):
        s = mod(plane + o, 2 * NP)
        arrived(rh.at[s], qh.at[s])
    rh[plane] = hb[plane]
    acc = jnp.zeros((32, DH), F32)
    for i in range(2 * NP):
        acc = acc + rh[i].astype(F32)
    zs[...] = acc.astype(BF16)

    @pl.when(z != 0)
    def _():
        pltpu.make_async_remote_copy(
            src_ref=zs, dst_ref=rz.at[z], send_sem=sz.at[0], recv_sem=qz.at[z],
            device_id=(p, y), device_id_type=MESH).start()

    dests = [mod(z + (f - 1) * FAR, NZ) for f in range(3)]
    ranks = [sum((other < d).astype(jnp.int32) for other in dests) for d in dests]
    for k in range(3):
        f = sum(jnp.where(r == k, i, 0) for i, r in enumerate(ranks))
        zd = mod(z + (f - 1) * FAR, NZ)
        for jn in range(4):
            arrived(r1.at[jn, f], q1.at[jn, f])

        @pl.when(f == 0)
        def _():
            arrived(r1.at[4, 0, :, vv], q1.at[4, 0])

        @pl.when(f == 2)
        def _():
            arrived(r1.at[4, 2, :, kk], q1.at[4, 2])

        total = tb[pl.ds(2 * zd, 2)].astype(F32)
        for jn in range(5):
            total = total + r1[jn, f].astype(F32)
        cs[f] = total.astype(BF16)

        @pl.when(f != 1)
        def _():
            pltpu.make_async_remote_copy(
                src_ref=cs.at[f, y], dst_ref=r2.at[f, 0], send_sem=s2.at[f, 0], recv_sem=q2.at[f, 0],
                device_id=(p, zd * 2 + y), device_id_type=MESH).start()

        pltpu.make_async_remote_copy(
            src_ref=cs.at[f, yo], dst_ref=r2.at[f, 1], send_sem=s2.at[f, 1], recv_sem=q2.at[f, 1],
            device_id=(p, zd * 2 + yo), device_id_type=MESH).start()

    def head_copies():
        out = []
        for dz in (0, 1, -1, 2, -2, 3, -3, 4, -4, 5, -5, 6, -6, 7, -7, 8):
            for w, yy in enumerate((y, yo)):
                if dz == 0 and w == 0:
                    continue
                out.append(pltpu.make_async_remote_copy(
                    src_ref=rg.at[y], dst_ref=rg.at[y], send_sem=sg.at[len(out)], recv_sem=qg.at[y],
                    device_id=(p, at(dz, yy)), device_id_type=MESH))
        return out

    kt[...] = ka[...].T

    def query_grad(h, _):
        cols = pl.ds(pl.multiple_of(h * RESP, RESP), RESP)
        acc = jnp.dot(kt[...], ds_s[:, cols], preferred_element_type=F32)
        dq_out[0, 0, :, pl.ds(pl.multiple_of(h * DH, DH), DH)] = (acc * SCALE).T.astype(BF16)
        return 0

    lax.fori_loop(0, H, query_grad, 0)

    @pl.when(z == 0)
    def _():
        total = acc
        for i in range(1, NZ):
            arrived(rz.at[i], qz.at[i])
        for i in range(1, NZ):
            total = total + rz[i].astype(F32)
        rg[y] = total
        for i, c in enumerate(head_copies()):
            c.start()

    for f in range(3):
        for w in range(2):
            if f == 1 and w == 0:
                continue
            arrived(r2.at[f, w], q2.at[f, w])
    total = cs[1, y].astype(F32) + r2[1, 1].astype(F32)
    for f in (0, 2):
        for w in range(2):
            total = total + r2[f, w].astype(F32)
    tkg_out[0] = total[:32]
    tvg_out[0] = total[32:]

    arrived(rg.at[yo], qg.at[yo])

    @pl.when(z != 0)
    def _():
        arrived(rg.at[y], qg.at[y])

    for w in range(2):
        hkg_out[w * 16 : (w + 1) * 16, :] = rg[w, :16, :]
        hvg_out[w * 16 : (w + 1) * 16, :] = rg[w, 16:, :]

    for c in sent:
        c.wait_send()
    for zd in range(NZ):
        one, two, whole, low, high = near_copies(zd)

        @pl.when(one)
        def _():
            whole.wait_send()

        @pl.when(two)
        def _():
            low.wait_send()
            high.wait_send()

    for f in range(3):
        for w in range(2):
            if f == 1 and w == 0:
                continue
            pltpu.make_async_remote_copy(
                src_ref=cs.at[f, w], dst_ref=r2.at[f, w], send_sem=s2.at[f, w], recv_sem=q2.at[f, w],
                device_id=(p, at(1, y)), device_id_type=MESH).wait_send()

    @pl.when(z != 0)
    def _():
        pltpu.make_async_remote_copy(
            src_ref=zs, dst_ref=rz.at[z], send_sem=sz.at[0], recv_sem=qz.at[z],
            device_id=(p, y), device_id_type=MESH).wait_send()

    @pl.when(z == 0)
    def _():
        for c in head_copies():
            c.wait_send()


def finish_kernel(*refs):
    ins, outs, sem = refs[:7], refs[7:14], refs[14]
    copies = [pltpu.make_async_copy(a, o, sem.at[i]) for i, (a, o) in enumerate(zip(ins, outs))]
    for c in copies:
        c.start()
    for c in copies:
        c.wait()


def per_device(q, rk, rv, tk, tv, hk, hv, g, lengths, forks):
    vm = pl.BlockSpec(memory_space=pltpu.VMEM)
    hbm = pl.BlockSpec(memory_space=pltpu.HBM)
    dma = pltpu.SemaphoreType.DMA
    sds = jax.ShapeDtypeStruct
    V = pltpu.VMEM
    shapes = (
            sds((1, 1, RESP, H * DH), BF16), sds((1, 1, RESP, DH), BF16), sds((1, 1, RESP, DH), BF16),
            sds((1, 32, DH), F32), sds((1, 32, DH), F32), sds((32, DH), F32), sds((32, DH), F32),
    )
    args = [
        pltpu.with_memory_space_constraint(a, pltpu.HBM)
        for a in (q, rk, rv, tk, tv, hk, hv, g)]
    raw = pl.pallas_call(
        kernel,
        out_shape=shapes,
        in_specs=[hbm] * 10,
        out_specs=(vm,) * 7,
        scratch_shapes=[
            V((H * RESP, DH), BF16), V((H * RESP, DH), BF16),
            V((H, DH, RESP), BF16), V((H, DH, RESP), BF16),
            V((KEYS, DH), BF16), V((KEYS, DH), BF16), V((DH, KEYS), BF16),
            V((NP, 64, DH), BF16), V((NB, 64, DH), BF16),
            V((H, KEYS, RESP), F32), V((H, KEYS, RESP), F32), V((KEYS, H * RESP), BF16),
            V((H, 1, RESP), F32), V((H, 8, RESP), F32), V((H, 8, RESP), F32),
            V((NZ + 3, H, 1, RESP), F32), V((NZ + 3, H, 1, RESP), F32), V((H, 1, RESP), F32),
            V((NB, 64, DH), BF16), V((5, 3, 2, 64, DH), BF16),
            V((3, 2, 64, DH), BF16), V((3, 2, 64, DH), BF16),
            V((2 * NP, 32, DH), BF16), V((2 * NP, 32, DH), BF16),
            V((32, DH), BF16), V((NZ, 32, DH), BF16), V((2, 32, DH), F32),
            pltpu.SMEM((1, 1), jnp.int32), pltpu.SMEM((1, 1), jnp.int32),
            dma((4 + 2 * H,)), dma((4,)),
            dma((48,)), dma((NP,)), dma((NB,)), dma((2,)),
            dma((NZ + 1,)), dma((5, 3)),
            dma((3, 2)), dma((3, 2)),
            dma((31,)), dma((32,)), dma((1,)), dma((NZ,)), dma((31,)), dma((2,)),
        ],
        compiler_params=pltpu.CompilerParams(
            collective_id=0, has_side_effects=True, vmem_limit_bytes=52 << 20),
    )(lengths, forks, *args)
    return pl.pallas_call(
        finish_kernel,
        out_shape=shapes,
        in_specs=(vm,) * 7,
        out_specs=(hbm,) * 7,
        scratch_shapes=[dma((7,))],
    )(*raw)


def solution(mesh):
    four, three, two = P("prompt", "branch", None, None), P("prompt", "branch", None), P("prompt", None)
    both = P("prompt", "branch")
    return jax.shard_map(
        per_device,
        mesh=mesh,
        in_specs=(four, four, four, three, three, two, two, four, both, both),
        out_specs=(four, four, four, three, three, two, two),
        check_vma=False,
    )
```

```python
import functools

import jax
import jax.numpy as jnp
from jax import lax
from jax.experimental import pallas as pl
from jax.experimental.pallas import tpu as pltpu
from jax.sharding import PartitionSpec as P

DH = 128
H = 8
BLK = 128
RESP = 256
HDR = 512
PREF = 1024
NP = 16
NB = 32
NZ = 16
CH = 256
KEYS = HDR + PREF + RESP
NCH = KEYS // CH
GATHER_STEP, GATHER_FARS = 3, 2
STEP, FARS = 5, 1
NEAR_MAX = STEP // 2
SPOKES = 2 * FARS + 1
REST = NZ // 2 - FARS * STEP
G_NEAR_MAX = GATHER_STEP // 2
G_REST = NZ // 2 - GATHER_FARS * GATHER_STEP
NEAR = tuple(j for j in range(-G_NEAR_MAX, G_NEAR_MAX + 1) if j != 0)
FAR = tuple(k * GATHER_STEP for k in range(-GATHER_FARS, GATHER_FARS + 1) if k != 0)
LOW = -1e30
SCALE = DH**-0.5
LOG2E = 1.4426950408889634
C2 = SCALE * LOG2E
UNROLL = 8
MESH = pl.DeviceIdType.MESH
F32 = jnp.float32
BF16 = jnp.bfloat16


def mod(a, n):
    return lax.rem(a + 4 * n, n)


def kernel(
    lengths, forks, q_hbm, rk_hbm, rv_hbm, tk_hbm, tv_hbm, hk_hbm, hv_hbm, g_hbm,
    dq_out, rkg_out, rvg_out, tkg_out, tvg_out, hkg_out, hvg_out,
    qf, gf, qt, gt, ka, va, kt, hkv, tkv, e_s, dp_s, ds_s, m_s, l_s, d_s, mb_s, fac_s, del_s,
    tb, r1, cs, r2, hb, rh, zs, rz, rg,
    in_sem, own_sem, gs, hrs, trs, ars, s1, q1, s2, q2, sh, qh, sz, qz, sg, qg,
):
    p = lax.axis_index("prompt")
    b = lax.axis_index("branch")
    z = b // 2
    y = lax.rem(b, 2)
    yo = 1 - y
    plane = p * 2 + y

    def at(dz, yy):
        return mod(z + dz, NZ) * 2 + yy

    own = [
        pltpu.make_async_copy(hk_hbm, hkv.at[p, pl.ds(0, 32)], own_sem.at[0]),
        pltpu.make_async_copy(hv_hbm, hkv.at[p, pl.ds(32, 32)], own_sem.at[1]),
        pltpu.make_async_copy(tk_hbm.at[0], tkv.at[b, pl.ds(0, 32)], own_sem.at[2]),
        pltpu.make_async_copy(tv_hbm.at[0], tkv.at[b, pl.ds(32, 32)], own_sem.at[3]),
    ]
    for c in own:
        c.start()
    barrier = pltpu.get_barrier_semaphore()
    greet = [(p, at(k, y)) for k in FAR]
    greet += [(p, at(j, yy)) for j in sorted({*NEAR, -G_REST, G_REST}) for yy in (y, yo)]
    greet += [(p, at(0, yo))]
    greet += [(mod(p + o, NP), b) for o in range(1, NP)]
    for d in greet:
        pl.semaphore_signal(barrier, 1, device_id=d, device_id_type=MESH)

    loads = [
        pltpu.make_async_copy(rk_hbm.at[0, 0], ka.at[pl.ds(HDR + PREF, RESP)], in_sem.at[0]),
        pltpu.make_async_copy(rv_hbm.at[0, 0], va.at[pl.ds(HDR + PREF, RESP)], in_sem.at[1]),
    ]
    for h in range(H):
        loads.append(pltpu.make_async_copy(
            q_hbm.at[0, 0, :, pl.ds(h * DH, DH)], qf.at[pl.ds(h * RESP, RESP)], in_sem.at[2 + h]))
        loads.append(pltpu.make_async_copy(
            g_hbm.at[0, 0, :, pl.ds(h * DH, DH)], gf.at[pl.ds(h * RESP, RESP)], in_sem.at[2 + H + h]))
    for c in loads:
        c.start()

    for c in own:
        c.wait()
    pl.semaphore_wait(barrier, len(greet))

    sent = []

    def send(src, dst, ssem, rsem, dev):
        c = pltpu.make_async_remote_copy(
            src_ref=src, dst_ref=dst, send_sem=ssem, recv_sem=rsem, device_id=dev, device_id_type=MESH)
        c.start()
        sent.append(c)

    n = 0
    slots = [b] + [at(k, y) for k in FAR]
    for k in sorted(FAR, key=abs, reverse=True):
        send(tkv.at[b], tkv.at[b], gs.at[n], trs.at[b], (p, at(k, y)))
        n += 1
    near = [at(j, yy) for j in NEAR for yy in (y, yo)] + [at(0, yo)]
    for d in near:
        send(tkv.at[b], tkv.at[b], gs.at[n], trs.at[b], (p, d))
        n += 1
    for o in range(1, NP):
        send(hkv.at[p], hkv.at[p], gs.at[n], hrs.at[p], (mod(p + o, NP), b))
        n += 1

    for c in loads:
        c.wait()
    live = lax.broadcasted_iota(jnp.int32, (RESP, DH), 0) < lengths[0, 0]

    def prepare(h, _):
        rows = pl.ds(pl.multiple_of(h * RESP, RESP), RESP)
        g = jnp.where(live, gf[rows, :], jnp.zeros((), BF16))
        gf[rows, :] = g
        gt[h] = g.T
        qt[h] = qf[rows, :].T
        m_s[h] = jnp.full((1, RESP), LOW, F32)
        l_s[h] = jnp.zeros((8, RESP), F32)
        d_s[h] = jnp.zeros((8, RESP), F32)
        return 0

    lax.fori_loop(0, H, prepare, 0)
    r1[2 * NEAR_MAX, 0, :, :32, :] = jnp.zeros((2, 32, DH), BF16)
    for f in range(1, 2 * FARS):
        r1[2 * NEAR_MAX, f] = jnp.zeros((2, 64, DH), BF16)
    r1[2 * NEAR_MAX, 2 * FARS, :, 32:, :] = jnp.zeros((2, 32, DH), BF16)
    fork = forks[0, 0]

    def stats(h, spots, seen, kind):
        keys = [ka[pl.ds(r, c), :] for r, c in spots]
        vals = [va[pl.ds(r, c), :] for r, c in spots]
        keys = keys[0] if len(keys) == 1 else jnp.concatenate(keys, axis=0)
        vals = vals[0] if len(vals) == 1 else jnp.concatenate(vals, axis=0)
        s = jnp.dot(keys, qt[h], preferred_element_type=F32)
        dp = jnp.dot(vals, gt[h], preferred_element_type=F32)
        if kind == "resp":
            key = lax.broadcasted_iota(jnp.int32, s.shape, 0)
            pos = lax.broadcasted_iota(jnp.int32, s.shape, 1)
            s = jnp.where(key <= pos, s, LOW)
        m_old = m_s[h]
        m_new = m_old
        first = 0
        for (r, c), see in zip(spots, seen):
            top = jnp.max(s[first : first + c], axis=0, keepdims=True)
            m_new = jnp.maximum(m_new, top if see is None else jnp.where(see, top, LOW))
            first += c
        f = jnp.exp2((m_old - m_new) * C2)
        shift = m_new * C2
        l = l_s[h] * f
        d = d_s[h] * f
        first = 0
        for (r, c), see in zip(spots, seen):
            move = shift if see is None else jnp.where(see, shift, -LOW)
            e = jnp.exp2(s[first : first + c] * C2 - move)
            dpu = dp[first : first + c]
            l = l + jnp.sum(e.reshape(c // 8, 8, RESP), axis=0)
            d = d + jnp.sum((e * dpu).reshape(c // 8, 8, RESP), axis=0)
            e_s[h, pl.ds(r, c), :] = e
            dp_s[h, pl.ds(r, c), :] = dpu
            first += c
        l_s[h] = l
        d_s[h] = d
        m_s[h] = m_new
        return m_new

    def stats_of(spots, seen, kind, marks):
        def body(h, _):
            m = stats(h, spots, seen, kind)
            for k in marks:
                mb_s[k, h] = m
            return 0
        lax.fori_loop(0, H, body, 0, unroll=UNROLL)

    def trunk_stats(zs_here):
        for zb in zs_here:
            for w in range(2):
                r = pl.ds(pl.multiple_of(HDR + zb * 64 + w * 32, 32), 32)
                ka[r, :] = tkv[2 * zb + w, :32, :]
                va[r, :] = tkv[2 * zb + w, 32:, :]
        spots = [(pl.multiple_of(HDR + zb * 64, 64), 64) for zb in zs_here]
        seen = [jnp.broadcast_to(zb // 2, (1, RESP)) < fork for zb in zs_here]
        stats_of(spots, seen, "trunk", zs_here)

    stats_of([(HDR + PREF, RESP)], [None], "resp", [NZ + 2])

    def arrived(ref, sem):
        pltpu.make_async_remote_copy(
            src_ref=ref, dst_ref=ref, send_sem=gs.at[0], recv_sem=sem,
            device_id=(p, at(1, y)), device_id_type=MESH).wait_recv()

    kk, vv = pl.ds(0, 32), pl.ds(32, 32)
    for k in sorted(FAR, key=abs):
        s = at(k, y)
        arrived(tkv.at[s], trs.at[s])
        for d in near:
            send(tkv.at[s], tkv.at[s], gs.at[n], trs.at[s], (p, d))
            n += 1
    first, last = at(FAR[0], y), at(FAR[-1], y)
    for yy in (y, yo):
        send(tkv.at[first, kk], tkv.at[first, kk], gs.at[n], trs.at[first], (p, at(G_REST, yy)))
        n += 1
        send(tkv.at[last, vv], tkv.at[last, vv], gs.at[n], ars.at[y], (p, at(-G_REST, yy)))
        n += 1

    for o in range(1, NP):
        s = mod(p + o, NP)
        arrived(hkv.at[s], hrs.at[s])
    for i in range(NP):
        ka[pl.ds(i * 32, 32), :] = hkv[i, :32, :]
        va[pl.ds(i * 32, 32), :] = hkv[i, 32:, :]

    def head_stats(i, _):
        stats_of([(pl.multiple_of(i * CH, CH), CH)], [None], "head", [NZ + i])
        return 0

    lax.fori_loop(0, HDR // CH, head_stats, 0)

    def group(j):
        return [mod(z + j + k, NZ) for k in sorted((0, *FAR), key=abs)]

    for zb in group(0):
        arrived(tkv.at[2 * zb + yo], trs.at[2 * zb + yo])
    trunk_stats(group(0))

    def near_group(k, _):
        j = ((k + 1) // 2) * (2 * lax.rem(k, 2) - 1)
        for zb in group(j):
            for yy in (y, yo):
                arrived(tkv.at[2 * zb + yy], trs.at[2 * zb + yy])
        trunk_stats(group(j))
        return 0

    lax.fori_loop(1, 2 * G_NEAR_MAX + 1, near_group, 0)
    anti = mod(z + 8, NZ)
    for yy in (y, yo):
        arrived(tkv.at[2 * anti + yy, kk], trs.at[2 * anti + yy])
        arrived(tkv.at[2 * anti + yy, vv], ars.at[yy])
    trunk_stats([anti])

    def finish(h, _):
        inv = 1.0 / jnp.sum(l_s[h], axis=0, keepdims=True)
        del_s[h] = jnp.sum(d_s[h], axis=0, keepdims=True) * inv
        m = m_s[h]
        for i in range(NZ + 3):
            fac_s[i, h] = jnp.exp2((mb_s[i, h] - m) * C2) * inv
        return 0

    lax.fori_loop(0, H, finish, 0)

    def terms(first, marks):
        rows = pl.ds(first, CH)
        c = CH // len(marks)
        kg = jnp.zeros((CH, DH), F32)
        vg = jnp.zeros((CH, DH), F32)
        for h in range(H):
            pr = [e_s[h, pl.ds(first + u * c, c), :] * fac_s[k, h] for u, k in enumerate(marks)]
            pr = pr[0] if len(pr) == 1 else jnp.concatenate(pr, axis=0)
            ds = (pr * (dp_s[h, rows, :] - del_s[h])).astype(BF16)
            ds_s[rows, h * RESP : (h + 1) * RESP] = ds
            kg = kg + jnp.dot(ds, qf[h * RESP : (h + 1) * RESP, :], preferred_element_type=F32)
            vg = vg + jnp.dot(pr.astype(BF16), gf[h * RESP : (h + 1) * RESP, :], preferred_element_type=F32)
        return kg * SCALE, vg

    def head_copy(q):
        return pltpu.make_async_remote_copy(
            src_ref=hb.at[q], dst_ref=rh.at[plane], send_sem=sh.at[q], recv_sem=qh.at[plane],
            device_id=(q // 2, z * 2 + lax.rem(q, 2)), device_id_type=MESH)

    def head_terms(i, _):
        kg, vg = terms(pl.multiple_of(i * CH, CH), [NZ + i])
        kg, vg = kg.astype(BF16), vg.astype(BF16)
        for u in range(CH // 16):
            hb[i * (CH // 16) + u, :16, :] = kg[u * 16 : (u + 1) * 16]
            hb[i * (CH // 16) + u, 16:, :] = vg[u * 16 : (u + 1) * 16]
        return 0

    lax.fori_loop(0, HDR // CH, head_terms, 0)
    for o in range(1, 2 * NP):
        head_copy(mod(plane + o, 2 * NP)).start()

    def route(zd):
        o = mod(zd - z, NZ)
        signed = jnp.where(o > NZ // 2, o - NZ, o)
        f = (signed + NEAR_MAX + FARS * STEP) // STEP
        j = signed - (f - FARS) * STEP
        jn = jnp.where(j < 0, j + NEAR_MAX, j + NEAR_MAX - 1)
        ok = jnp.logical_and(o != NZ // 2, j != 0)
        return o, ok, jnp.where(ok, j, 1), jnp.where(ok, jn, 0), jnp.where(ok, f, 0)

    def near_copies(zd):
        o, ok, j, jn, f = route(zd)
        whole = pltpu.make_async_remote_copy(
            src_ref=tb.at[pl.ds(2 * zd, 2)], dst_ref=r1.at[jn, f], send_sem=s1.at[zd], recv_sem=q1.at[jn, f],
            device_id=(p, mod(z + j, NZ) * 2 + y), device_id_type=MESH)
        low = pltpu.make_async_remote_copy(
            src_ref=tb.at[pl.ds(2 * zd, 2), kk], dst_ref=r1.at[2 * NEAR_MAX, 2 * FARS, :, kk],
            send_sem=s1.at[zd], recv_sem=q1.at[2 * NEAR_MAX, 2 * FARS],
            device_id=(p, at(REST, y)), device_id_type=MESH)
        high = pltpu.make_async_remote_copy(
            src_ref=tb.at[pl.ds(2 * zd, 2), vv], dst_ref=r1.at[2 * NEAR_MAX, 0, :, vv],
            send_sem=s1.at[NZ], recv_sem=q1.at[2 * NEAR_MAX, 0],
            device_id=(p, at(-REST, y)), device_id_type=MESH)
        return ok, o == NZ // 2, whole, low, high

    def trunk_terms(i, _):
        kg, vg = terms(pl.multiple_of(HDR + i * CH, CH), [i * 4 + u for u in range(4)])
        kg, vg = kg.astype(BF16), vg.astype(BF16)
        for u in range(CH // 32):
            k = i * (CH // 32) + u
            tb[k, :32, :] = kg[u * 32 : (u + 1) * 32]
            tb[k, 32:, :] = vg[u * 32 : (u + 1) * 32]
        for u in range(4):
            one, two, whole, low, high = near_copies(i * 4 + u)

            @pl.when(one)
            def _():
                whole.start()

            @pl.when(two)
            def _():
                low.start()
                high.start()
        return 0

    lax.fori_loop(0, PREF // CH, trunk_terms, 0)

    kg, vg = terms(HDR + PREF, [NZ + 2])
    rkg_out[0, 0] = kg.astype(BF16)
    rvg_out[0, 0] = vg.astype(BF16)

    for o in range(1, 2 * NP):
        s = mod(plane + o, 2 * NP)
        arrived(rh.at[s], qh.at[s])
    rh[plane] = hb[plane]
    acc = jnp.zeros((32, DH), F32)
    for i in range(2 * NP):
        acc = acc + rh[i].astype(F32)
    zs[...] = acc.astype(BF16)

    @pl.when(z != 0)
    def _():
        pltpu.make_async_remote_copy(
            src_ref=zs, dst_ref=rz.at[z], send_sem=sz.at[0], recv_sem=qz.at[z],
            device_id=(p, y), device_id_type=MESH).start()

    dests = [mod(z + (f - FARS) * STEP, NZ) for f in range(SPOKES)]
    ranks = [sum((other < d).astype(jnp.int32) for other in dests) for d in dests]
    for k in range(SPOKES):
        f = sum(jnp.where(r == k, i, 0) for i, r in enumerate(ranks))
        zd = mod(z + (f - FARS) * STEP, NZ)
        for jn in range(2 * NEAR_MAX):
            arrived(r1.at[jn, f], q1.at[jn, f])

        @pl.when(f == 0)
        def _():
            arrived(r1.at[2 * NEAR_MAX, 0, :, vv], q1.at[2 * NEAR_MAX, 0])

        @pl.when(f == 2 * FARS)
        def _():
            arrived(r1.at[2 * NEAR_MAX, 2 * FARS, :, kk], q1.at[2 * NEAR_MAX, 2 * FARS])

        total = tb[pl.ds(2 * zd, 2)].astype(F32)
        for jn in range(2 * NEAR_MAX + 1):
            total = total + r1[jn, f].astype(F32)
        cs[f] = total.astype(BF16)

        @pl.when(f != FARS)
        def _():
            pltpu.make_async_remote_copy(
                src_ref=cs.at[f, y], dst_ref=r2.at[f, 0], send_sem=s2.at[f, 0], recv_sem=q2.at[f, 0],
                device_id=(p, zd * 2 + y), device_id_type=MESH).start()

        pltpu.make_async_remote_copy(
            src_ref=cs.at[f, yo], dst_ref=r2.at[f, 1], send_sem=s2.at[f, 1], recv_sem=q2.at[f, 1],
            device_id=(p, zd * 2 + yo), device_id_type=MESH).start()

    def head_copies():
        out = []
        for dz in (0, 1, -1, 2, -2, 3, -3, 4, -4, 5, -5, 6, -6, 7, -7, 8):
            for w, yy in enumerate((y, yo)):
                if dz == 0 and w == 0:
                    continue
                out.append(pltpu.make_async_remote_copy(
                    src_ref=rg.at[y], dst_ref=rg.at[y], send_sem=sg.at[len(out)], recv_sem=qg.at[y],
                    device_id=(p, at(dz, yy)), device_id_type=MESH))
        return out

    kt[...] = ka[...].T

    def query_grad(h, _):
        cols = pl.ds(pl.multiple_of(h * RESP, RESP), RESP)
        acc = jnp.dot(kt[...], ds_s[:, cols], preferred_element_type=F32)
        dq_out[0, 0, :, pl.ds(pl.multiple_of(h * DH, DH), DH)] = (acc * SCALE).T.astype(BF16)
        return 0

    lax.fori_loop(0, H, query_grad, 0)

    for c in sent:
        c.wait_send()
    for zd in range(NZ):
        one, two, whole, low, high = near_copies(zd)

        @pl.when(one)
        def _():
            whole.wait_send()

        @pl.when(two)
        def _():
            low.wait_send()
            high.wait_send()

    for q in range(2 * NP):

        @pl.when(q != plane)
        def _():
            head_copy(q).wait_send()

    @pl.when(z == 0)
    def _():
        total = acc
        for i in range(1, NZ):
            arrived(rz.at[i], qz.at[i])
        for i in range(1, NZ):
            total = total + rz[i].astype(F32)
        rg[y] = total.astype(BF16)
        for i, c in enumerate(head_copies()):
            c.start()

    spokes = [(f, w) for f in range(SPOKES) for w in range(2) if (f, w) != (FARS, 0)]
    for f, w in spokes:
        arrived(r2.at[f, w], q2.at[f, w])
    total = cs[FARS, y].astype(F32)
    for f, w in spokes:
        total = total + r2[f, w].astype(F32)
    tkg_out[0] = total[:32]
    tvg_out[0] = total[32:]

    arrived(rg.at[yo], qg.at[yo])

    @pl.when(z != 0)
    def _():
        arrived(rg.at[y], qg.at[y])

    for w in range(2):
        hkg_out[w * 16 : (w + 1) * 16, :] = rg[w, :16, :].astype(F32)
        hvg_out[w * 16 : (w + 1) * 16, :] = rg[w, 16:, :].astype(F32)

    for f, w in spokes:
        pltpu.make_async_remote_copy(
            src_ref=cs.at[f, w], dst_ref=r2.at[f, w], send_sem=s2.at[f, w], recv_sem=q2.at[f, w],
            device_id=(p, at(1, y)), device_id_type=MESH).wait_send()
    @pl.when(z != 0)
    def _():
        pltpu.make_async_remote_copy(
            src_ref=zs, dst_ref=rz.at[z], send_sem=sz.at[0], recv_sem=qz.at[z],
            device_id=(p, y), device_id_type=MESH).wait_send()

    @pl.when(z == 0)
    def _():
        for c in head_copies():
            c.wait_send()


def finish_kernel(*refs):
    ins, outs, sem = refs[:7], refs[7:14], refs[14]
    copies = [pltpu.make_async_copy(a, o, sem.at[i]) for i, (a, o) in enumerate(zip(ins, outs))]
    for c in copies:
        c.start()
    for c in copies:
        c.wait()


def per_device(q, rk, rv, tk, tv, hk, hv, g, lengths, forks):
    vm = pl.BlockSpec(memory_space=pltpu.VMEM)
    hbm = pl.BlockSpec(memory_space=pltpu.HBM)
    smem = pl.BlockSpec(memory_space=pltpu.SMEM)
    dma = pltpu.SemaphoreType.DMA
    sds = jax.ShapeDtypeStruct
    V = pltpu.VMEM
    shapes = (
            sds((1, 1, RESP, H * DH), BF16), sds((1, 1, RESP, DH), BF16), sds((1, 1, RESP, DH), BF16),
            sds((1, 32, DH), F32), sds((1, 32, DH), F32), sds((32, DH), F32), sds((32, DH), F32),
    )
    args = [
        pltpu.with_memory_space_constraint(a, pltpu.HBM)
        for a in (q, rk, rv, tk, tv, hk, hv, g)]
    raw = pl.pallas_call(
        kernel,
        out_shape=shapes,
        in_specs=[smem, smem] + [hbm] * 8,
        out_specs=(vm,) * 7,
        scratch_shapes=[
            V((H * RESP, DH), BF16), V((H * RESP, DH), BF16),
            V((H, DH, RESP), BF16), V((H, DH, RESP), BF16),
            V((KEYS, DH), BF16), V((KEYS, DH), BF16), V((DH, KEYS), BF16),
            V((NP, 64, DH), BF16), V((NB, 64, DH), BF16),
            V((H, KEYS, RESP), F32), V((H, KEYS, RESP), F32), V((KEYS, H * RESP), BF16),
            V((H, 1, RESP), F32), V((H, 8, RESP), F32), V((H, 8, RESP), F32),
            V((NZ + 3, H, 1, RESP), F32), V((NZ + 3, H, 1, RESP), F32), V((H, 1, RESP), F32),
            V((NB, 64, DH), BF16), V((2 * NEAR_MAX + 1, SPOKES, 2, 64, DH), BF16),
            V((SPOKES, 2, 64, DH), BF16), V((SPOKES, 2, 64, DH), BF16),
            V((2 * NP, 32, DH), BF16), V((2 * NP, 32, DH), BF16),
            V((32, DH), BF16), V((NZ, 32, DH), BF16), V((2, 32, DH), BF16),
            dma((2 + 2 * H,)), dma((4,)),
            dma((48,)), dma((NP,)), dma((NB,)), dma((2,)),
            dma((NZ + 1,)), dma((2 * NEAR_MAX + 1, SPOKES)),
            dma((SPOKES, 2)), dma((SPOKES, 2)),
            dma((32,)), dma((32,)), dma((1,)), dma((NZ,)), dma((31,)), dma((2,)),
        ],
        compiler_params=pltpu.CompilerParams(
            collective_id=0, has_side_effects=True, vmem_limit_bytes=52 << 20),
    )(lengths, forks, *args)
    return pl.pallas_call(
        finish_kernel,
        out_shape=shapes,
        in_specs=(vm,) * 7,
        out_specs=(hbm,) * 7,
        scratch_shapes=[dma((7,))],
    )(*[pltpu.with_memory_space_constraint(a, pltpu.VMEM) for a in raw])


def solution(mesh):
    four, three, two = P("prompt", "branch", None, None), P("prompt", "branch", None), P("prompt", None)
    both = P("prompt", "branch")
    return jax.shard_map(
        per_device,
        mesh=mesh,
        in_specs=(four, four, four, three, three, two, two, four, both, both),
        out_specs=(four, four, four, three, three, two, two),
        check_vma=False,
    )
```

```python
import functools

import jax
import jax.numpy as jnp
from jax import lax
from jax.experimental import pallas as pl
from jax.experimental.pallas import tpu as pltpu
from jax.sharding import PartitionSpec as P

DH = 128
H = 8
BLK = 128
RESP = 256
HDR = 512
PREF = 1024
NP = 16
NB = 32
NZ = 16
CH = 256
KEYS = HDR + PREF + RESP
NCH = KEYS // CH
GATHER_STEP, GATHER_FARS = 3, 2
STEP, FARS = 5, 1
NEAR_MAX = STEP // 2
SPOKES = 2 * FARS + 1
REST = NZ // 2 - FARS * STEP
G_NEAR_MAX = GATHER_STEP // 2
G_REST = NZ // 2 - GATHER_FARS * GATHER_STEP
NEAR = tuple(j for j in range(-G_NEAR_MAX, G_NEAR_MAX + 1) if j != 0)
FAR = tuple(k * GATHER_STEP for k in range(-GATHER_FARS, GATHER_FARS + 1) if k != 0)
LOW = -1e30
SCALE = DH**-0.5
LOG2E = 1.4426950408889634
C2 = SCALE * LOG2E
UNROLL = 8
MESH = pl.DeviceIdType.MESH
F32 = jnp.float32
BF16 = jnp.bfloat16


def mod(a, n):
    return lax.rem(a + 4 * n, n)


def kernel(
    lengths, forks, q_hbm, rk_hbm, rv_hbm, tk_hbm, tv_hbm, hk_hbm, hv_hbm, g_hbm,
    dq_out, rkg_out, rvg_out, tkg_out, tvg_out, hkg_out, hvg_out,
    qf, gf, qt, gt, ka, va, kt, hkv, tkv, e_s, dp_s, ds_s, m_s, l_s, d_s, mb_s, fac_s, del_s,
    tb, r1, cs, r2, hb, rh, zs, rz, rg,
    in_sem, own_sem, gs, hrs, trs, ars, s1, q1, s2, q2, sh, qh, sz, qz, sg, qg,
):
    p = lax.axis_index("prompt")
    b = lax.axis_index("branch")
    z = b // 2
    y = lax.rem(b, 2)
    yo = 1 - y
    plane = p * 2 + y

    def at(dz, yy):
        return mod(z + dz, NZ) * 2 + yy

    own = [
        pltpu.make_async_copy(hk_hbm, hkv.at[p, pl.ds(0, 32)], own_sem.at[0]),
        pltpu.make_async_copy(hv_hbm, hkv.at[p, pl.ds(32, 32)], own_sem.at[1]),
        pltpu.make_async_copy(tk_hbm.at[0], tkv.at[b, pl.ds(0, 32)], own_sem.at[2]),
        pltpu.make_async_copy(tv_hbm.at[0], tkv.at[b, pl.ds(32, 32)], own_sem.at[3]),
    ]
    for c in own:
        c.start()
    barrier = pltpu.get_barrier_semaphore()
    greet = [(p, at(k, y)) for k in FAR]
    greet += [(p, at(j, yy)) for j in sorted({*NEAR, -G_REST, G_REST}) for yy in (y, yo)]
    greet += [(p, at(0, yo))]
    greet += [(mod(p + o, NP), b) for o in range(1, NP)]
    for d in greet:
        pl.semaphore_signal(barrier, 1, device_id=d, device_id_type=MESH)

    loads = [
        pltpu.make_async_copy(rk_hbm.at[0, 0], ka.at[pl.ds(HDR + PREF, RESP)], in_sem.at[0]),
        pltpu.make_async_copy(rv_hbm.at[0, 0], va.at[pl.ds(HDR + PREF, RESP)], in_sem.at[1]),
    ]
    for h in range(H):
        loads.append(pltpu.make_async_copy(
            q_hbm.at[0, 0, :, pl.ds(h * DH, DH)], qf.at[pl.ds(h * RESP, RESP)], in_sem.at[2 + h]))
        loads.append(pltpu.make_async_copy(
            g_hbm.at[0, 0, :, pl.ds(h * DH, DH)], gf.at[pl.ds(h * RESP, RESP)], in_sem.at[2 + H + h]))
    for c in loads:
        c.start()

    for c in own:
        c.wait()
    pl.semaphore_wait(barrier, len(greet))

    sent = []

    def send(src, dst, ssem, rsem, dev):
        c = pltpu.make_async_remote_copy(
            src_ref=src, dst_ref=dst, send_sem=ssem, recv_sem=rsem, device_id=dev, device_id_type=MESH)
        c.start()
        sent.append(c)

    n = 0
    slots = [b] + [at(k, y) for k in FAR]
    for k in sorted(FAR, key=abs, reverse=True):
        send(tkv.at[b], tkv.at[b], gs.at[n], trs.at[b], (p, at(k, y)))
        n += 1
    near = [at(j, yy) for j in NEAR for yy in (y, yo)] + [at(0, yo)]
    for d in near:
        send(tkv.at[b], tkv.at[b], gs.at[n], trs.at[b], (p, d))
        n += 1
    for o in range(1, NP):
        send(hkv.at[p], hkv.at[p], gs.at[n], hrs.at[p], (mod(p + o, NP), b))
        n += 1

    for c in loads:
        c.wait()
    live = lax.broadcasted_iota(jnp.int32, (RESP, DH), 0) < lengths[0, 0]

    def prepare(h, _):
        rows = pl.ds(pl.multiple_of(h * RESP, RESP), RESP)
        g = jnp.where(live, gf[rows, :], jnp.zeros((), BF16))
        gf[rows, :] = g
        gt[h] = g.T
        qt[h] = qf[rows, :].T
        m_s[h] = jnp.full((1, RESP), LOW, F32)
        l_s[h] = jnp.zeros((8, RESP), F32)
        d_s[h] = jnp.zeros((8, RESP), F32)
        return 0

    lax.fori_loop(0, H, prepare, 0)
    r1[2 * NEAR_MAX, 0, :, :32, :] = jnp.zeros((2, 32, DH), BF16)
    for f in range(1, 2 * FARS):
        r1[2 * NEAR_MAX, f] = jnp.zeros((2, 64, DH), BF16)
    r1[2 * NEAR_MAX, 2 * FARS, :, 32:, :] = jnp.zeros((2, 32, DH), BF16)
    fork = forks[0, 0]

    def stats(h, spots, seen, kind):
        keys = [ka[pl.ds(r, c), :] for r, c in spots]
        vals = [va[pl.ds(r, c), :] for r, c in spots]
        keys = keys[0] if len(keys) == 1 else jnp.concatenate(keys, axis=0)
        vals = vals[0] if len(vals) == 1 else jnp.concatenate(vals, axis=0)
        s = jnp.dot(keys, qt[h], preferred_element_type=F32)
        dp = jnp.dot(vals, gt[h], preferred_element_type=F32)
        if kind == "resp":
            key = lax.broadcasted_iota(jnp.int32, s.shape, 0)
            pos = lax.broadcasted_iota(jnp.int32, s.shape, 1)
            s = jnp.where(key <= pos, s, LOW)
        m_old = m_s[h]
        m_new = m_old
        first = 0
        for (r, c), see in zip(spots, seen):
            top = jnp.max(s[first : first + c], axis=0, keepdims=True)
            m_new = jnp.maximum(m_new, top if see is None else jnp.where(see, top, LOW))
            first += c
        f = jnp.exp2((m_old - m_new) * C2)
        shift = m_new * C2
        l = l_s[h] * f
        d = d_s[h] * f
        first = 0
        for (r, c), see in zip(spots, seen):
            move = shift if see is None else jnp.where(see, shift, -LOW)
            e = jnp.exp2(s[first : first + c] * C2 - move)
            dpu = dp[first : first + c]
            l = l + jnp.sum(e.reshape(c // 8, 8, RESP), axis=0)
            d = d + jnp.sum((e * dpu).reshape(c // 8, 8, RESP), axis=0)
            e_s[h, pl.ds(r, c), :] = e
            dp_s[h, pl.ds(r, c), :] = dpu
            first += c
        l_s[h] = l
        d_s[h] = d
        m_s[h] = m_new
        return m_new

    def stats_of(spots, seen, kind, marks):
        def body(h, _):
            m = stats(h, spots, seen, kind)
            for k in marks:
                mb_s[k, h] = m
            return 0
        lax.fori_loop(0, H, body, 0, unroll=UNROLL)

    def trunk_stats(zs_here):
        for zb in zs_here:
            for w in range(2):
                r = pl.ds(pl.multiple_of(HDR + zb * 64 + w * 32, 32), 32)
                ka[r, :] = tkv[2 * zb + w, :32, :]
                va[r, :] = tkv[2 * zb + w, 32:, :]
        spots = [(pl.multiple_of(HDR + zb * 64, 64), 64) for zb in zs_here]
        seen = [jnp.broadcast_to(zb // 2, (1, RESP)) < fork for zb in zs_here]
        stats_of(spots, seen, "trunk", zs_here)

    stats_of([(HDR + PREF, RESP)], [None], "resp", [NZ + 2])

    def arrived(ref, sem):
        pltpu.make_async_remote_copy(
            src_ref=ref, dst_ref=ref, send_sem=gs.at[0], recv_sem=sem,
            device_id=(p, at(1, y)), device_id_type=MESH).wait_recv()

    kk, vv = pl.ds(0, 32), pl.ds(32, 32)
    def pass_on(k, n):
        s = at(k, y)
        arrived(tkv.at[s], trs.at[s])
        for d in near:
            send(tkv.at[s], tkv.at[s], gs.at[n], trs.at[s], (p, d))
            n += 1
        return n

    def group(k):
        for yy in (y, yo):
            for j in NEAR:
                arrived(tkv.at[at(k + j, yy)], trs.at[at(k + j, yy)])
        arrived(tkv.at[at(k, yo)], trs.at[at(k, yo)])
        return [mod(z + k + j, NZ) for j in (0, *NEAR)]

    by_distance = sorted(FAR, key=abs)
    for k in by_distance:
        if abs(k) == GATHER_STEP:
            n = pass_on(k, n)
    trunk_stats(group(0))
    for k in by_distance:
        if abs(k) > GATHER_STEP:
            n = pass_on(k, n)
    first, last = at(FAR[0], y), at(FAR[-1], y)
    for yy in (y, yo):
        send(tkv.at[first, kk], tkv.at[first, kk], gs.at[n], trs.at[first], (p, at(G_REST, yy)))
        n += 1
        send(tkv.at[last, vv], tkv.at[last, vv], gs.at[n], ars.at[y], (p, at(-G_REST, yy)))
        n += 1

    for o in range(1, NP):
        s = mod(p + o, NP)
        arrived(hkv.at[s], hrs.at[s])
    for i in range(NP):
        ka[pl.ds(i * 32, 32), :] = hkv[i, :32, :]
        va[pl.ds(i * 32, 32), :] = hkv[i, 32:, :]

    def head_stats(i, _):
        stats_of([(pl.multiple_of(i * CH, CH), CH)], [None], "head", [NZ + i])
        return 0

    lax.fori_loop(0, HDR // CH, head_stats, 0)

    def far_group(i, _):
        k = (i // 2 + 1) * GATHER_STEP * (1 - 2 * lax.rem(i, 2))
        trunk_stats(group(k))
        return 0

    lax.fori_loop(0, 2 * GATHER_FARS - 1, far_group, 0)
    last_group = group(-GATHER_FARS * GATHER_STEP)
    anti = mod(z + 8, NZ)
    for yy in (y, yo):
        arrived(tkv.at[2 * anti + yy, kk], trs.at[2 * anti + yy])
        arrived(tkv.at[2 * anti + yy, vv], ars.at[yy])
    trunk_stats(last_group + [anti])

    def finish(h, _):
        inv = 1.0 / jnp.sum(l_s[h], axis=0, keepdims=True)
        del_s[h] = jnp.sum(d_s[h], axis=0, keepdims=True) * inv
        m = m_s[h]
        for i in range(NZ + 3):
            fac_s[i, h] = jnp.exp2((mb_s[i, h] - m) * C2) * inv
        return 0

    lax.fori_loop(0, H, finish, 0, unroll=UNROLL)

    def terms(first, marks):
        rows = pl.ds(first, CH)
        c = CH // len(marks)
        kg = jnp.zeros((CH, DH), F32)
        vg = jnp.zeros((CH, DH), F32)
        for h in range(H):
            pr = [e_s[h, pl.ds(first + u * c, c), :] * fac_s[k, h] for u, k in enumerate(marks)]
            pr = pr[0] if len(pr) == 1 else jnp.concatenate(pr, axis=0)
            ds = (pr * (dp_s[h, rows, :] - del_s[h])).astype(BF16)
            ds_s[rows, h * RESP : (h + 1) * RESP] = ds
            kg = kg + jnp.dot(ds, qf[h * RESP : (h + 1) * RESP, :], preferred_element_type=F32)
            vg = vg + jnp.dot(pr.astype(BF16), gf[h * RESP : (h + 1) * RESP, :], preferred_element_type=F32)
        return kg * SCALE, vg

    def head_copy(q):
        return pltpu.make_async_remote_copy(
            src_ref=hb.at[q], dst_ref=rh.at[plane], send_sem=sh.at[q], recv_sem=qh.at[plane],
            device_id=(q // 2, z * 2 + lax.rem(q, 2)), device_id_type=MESH)

    def head_terms(i, _):
        kg, vg = terms(pl.multiple_of(i * CH, CH), [NZ + i])
        kg, vg = kg.astype(BF16), vg.astype(BF16)
        for u in range(CH // 16):
            hb[i * (CH // 16) + u, :16, :] = kg[u * 16 : (u + 1) * 16]
            hb[i * (CH // 16) + u, 16:, :] = vg[u * 16 : (u + 1) * 16]
        return 0

    lax.fori_loop(0, HDR // CH, head_terms, 0)
    for o in range(1, 2 * NP):
        head_copy(mod(plane + o, 2 * NP)).start()

    def route(zd):
        o = mod(zd - z, NZ)
        signed = jnp.where(o > NZ // 2, o - NZ, o)
        f = (signed + NEAR_MAX + FARS * STEP) // STEP
        j = signed - (f - FARS) * STEP
        jn = jnp.where(j < 0, j + NEAR_MAX, j + NEAR_MAX - 1)
        ok = jnp.logical_and(o != NZ // 2, j != 0)
        return o, ok, jnp.where(ok, j, 1), jnp.where(ok, jn, 0), jnp.where(ok, f, 0)

    def near_copies(zd):
        o, ok, j, jn, f = route(zd)
        whole = pltpu.make_async_remote_copy(
            src_ref=tb.at[pl.ds(2 * zd, 2)], dst_ref=r1.at[jn, f], send_sem=s1.at[zd], recv_sem=q1.at[jn, f],
            device_id=(p, mod(z + j, NZ) * 2 + y), device_id_type=MESH)
        low = pltpu.make_async_remote_copy(
            src_ref=tb.at[pl.ds(2 * zd, 2), kk], dst_ref=r1.at[2 * NEAR_MAX, 2 * FARS, :, kk],
            send_sem=s1.at[zd], recv_sem=q1.at[2 * NEAR_MAX, 2 * FARS],
            device_id=(p, at(REST, y)), device_id_type=MESH)
        high = pltpu.make_async_remote_copy(
            src_ref=tb.at[pl.ds(2 * zd, 2), vv], dst_ref=r1.at[2 * NEAR_MAX, 0, :, vv],
            send_sem=s1.at[NZ], recv_sem=q1.at[2 * NEAR_MAX, 0],
            device_id=(p, at(-REST, y)), device_id_type=MESH)
        return ok, o == NZ // 2, whole, low, high

    def trunk_terms(i, _):
        kg, vg = terms(pl.multiple_of(HDR + i * CH, CH), [i * 4 + u for u in range(4)])
        kg, vg = kg.astype(BF16), vg.astype(BF16)
        for u in range(CH // 32):
            k = i * (CH // 32) + u
            tb[k, :32, :] = kg[u * 32 : (u + 1) * 32]
            tb[k, 32:, :] = vg[u * 32 : (u + 1) * 32]
        for u in range(4):
            one, two, whole, low, high = near_copies(i * 4 + u)

            @pl.when(one)
            def _():
                whole.start()

            @pl.when(two)
            def _():
                low.start()
                high.start()
        return 0

    lax.fori_loop(0, PREF // CH, trunk_terms, 0)

    for o in range(1, 2 * NP):
        s = mod(plane + o, 2 * NP)
        arrived(rh.at[s], qh.at[s])
    rh[plane] = hb[plane]
    acc = jnp.zeros((32, DH), F32)
    for i in range(2 * NP):
        acc = acc + rh[i].astype(F32)
    zs[...] = acc.astype(BF16)

    @pl.when(z != 0)
    def _():
        pltpu.make_async_remote_copy(
            src_ref=zs, dst_ref=rz.at[z], send_sem=sz.at[0], recv_sem=qz.at[z],
            device_id=(p, y), device_id_type=MESH).start()

    kg, vg = terms(HDR + PREF, [NZ + 2])
    rkg_out[0, 0] = kg.astype(BF16)
    rvg_out[0, 0] = vg.astype(BF16)

    kt[...] = ka[...].T

    def query_grad(h, _):
        cols = pl.ds(pl.multiple_of(h * RESP, RESP), RESP)
        acc = jnp.dot(kt[...], ds_s[:, cols], preferred_element_type=F32)
        dq_out[0, 0, :, pl.ds(pl.multiple_of(h * DH, DH), DH)] = (acc * SCALE).T.astype(BF16)
        return 0

    lax.fori_loop(0, H // 2, query_grad, 0)

    dests = [mod(z + (f - FARS) * STEP, NZ) for f in range(SPOKES)]
    ranks = [sum((other < d).astype(jnp.int32) for other in dests) for d in dests]
    for k in range(SPOKES):
        f = sum(jnp.where(r == k, i, 0) for i, r in enumerate(ranks))
        zd = mod(z + (f - FARS) * STEP, NZ)
        for jn in range(2 * NEAR_MAX):
            arrived(r1.at[jn, f], q1.at[jn, f])

        @pl.when(f == 0)
        def _():
            arrived(r1.at[2 * NEAR_MAX, 0, :, vv], q1.at[2 * NEAR_MAX, 0])

        @pl.when(f == 2 * FARS)
        def _():
            arrived(r1.at[2 * NEAR_MAX, 2 * FARS, :, kk], q1.at[2 * NEAR_MAX, 2 * FARS])

        total = tb[pl.ds(2 * zd, 2)].astype(F32)
        for jn in range(2 * NEAR_MAX + 1):
            total = total + r1[jn, f].astype(F32)
        cs[f] = total.astype(BF16)

        @pl.when(f != FARS)
        def _():
            pltpu.make_async_remote_copy(
                src_ref=cs.at[f, y], dst_ref=r2.at[f, 0], send_sem=s2.at[f, 0], recv_sem=q2.at[f, 0],
                device_id=(p, zd * 2 + y), device_id_type=MESH).start()

        pltpu.make_async_remote_copy(
            src_ref=cs.at[f, yo], dst_ref=r2.at[f, 1], send_sem=s2.at[f, 1], recv_sem=q2.at[f, 1],
            device_id=(p, zd * 2 + yo), device_id_type=MESH).start()

    def head_copies():
        out = []
        for dz in (0, 1, -1, 2, -2, 3, -3, 4, -4, 5, -5, 6, -6, 7, -7, 8):
            for w, yy in enumerate((y, yo)):
                if dz == 0 and w == 0:
                    continue
                out.append(pltpu.make_async_remote_copy(
                    src_ref=rg.at[y], dst_ref=rg.at[y], send_sem=sg.at[len(out)], recv_sem=qg.at[y],
                    device_id=(p, at(dz, yy)), device_id_type=MESH))
        return out

    lax.fori_loop(H // 2, H, query_grad, 0)

    @pl.when(z == 0)
    def _():
        total = acc
        for i in range(1, NZ):
            arrived(rz.at[i], qz.at[i])
        for i in range(1, NZ):
            total = total + rz[i].astype(F32)
        rg[y] = total.astype(BF16)
        for i, c in enumerate(head_copies()):
            c.start()

    for c in sent:
        c.wait_send()
    for zd in range(NZ):
        one, two, whole, low, high = near_copies(zd)

        @pl.when(one)
        def _():
            whole.wait_send()

        @pl.when(two)
        def _():
            low.wait_send()
            high.wait_send()

    for q in range(2 * NP):

        @pl.when(q != plane)
        def _():
            head_copy(q).wait_send()

    spokes = [(f, w) for f in range(SPOKES) for w in range(2) if (f, w) != (FARS, 0)]
    for f, w in spokes:
        arrived(r2.at[f, w], q2.at[f, w])
    total = cs[FARS, y].astype(F32)
    for f, w in spokes:
        total = total + r2[f, w].astype(F32)
    tkg_out[0] = total[:32]
    tvg_out[0] = total[32:]

    arrived(rg.at[yo], qg.at[yo])

    @pl.when(z != 0)
    def _():
        arrived(rg.at[y], qg.at[y])

    for w in range(2):
        hkg_out[w * 16 : (w + 1) * 16, :] = rg[w, :16, :].astype(F32)
        hvg_out[w * 16 : (w + 1) * 16, :] = rg[w, 16:, :].astype(F32)

    for f, w in spokes:
        pltpu.make_async_remote_copy(
            src_ref=cs.at[f, w], dst_ref=r2.at[f, w], send_sem=s2.at[f, w], recv_sem=q2.at[f, w],
            device_id=(p, at(1, y)), device_id_type=MESH).wait_send()
    @pl.when(z != 0)
    def _():
        pltpu.make_async_remote_copy(
            src_ref=zs, dst_ref=rz.at[z], send_sem=sz.at[0], recv_sem=qz.at[z],
            device_id=(p, y), device_id_type=MESH).wait_send()

    @pl.when(z == 0)
    def _():
        for c in head_copies():
            c.wait_send()


def finish_kernel(*refs):
    ins, outs, sem = refs[:7], refs[7:14], refs[14]
    copies = [pltpu.make_async_copy(a, o, sem.at[i]) for i, (a, o) in enumerate(zip(ins, outs))]
    for c in copies:
        c.start()
    for c in copies:
        c.wait()


def per_device(q, rk, rv, tk, tv, hk, hv, g, lengths, forks):
    vm = pl.BlockSpec(memory_space=pltpu.VMEM)
    hbm = pl.BlockSpec(memory_space=pltpu.HBM)
    smem = pl.BlockSpec(memory_space=pltpu.SMEM)
    dma = pltpu.SemaphoreType.DMA
    sds = jax.ShapeDtypeStruct
    V = pltpu.VMEM
    shapes = (
            sds((1, 1, RESP, H * DH), BF16), sds((1, 1, RESP, DH), BF16), sds((1, 1, RESP, DH), BF16),
            sds((1, 32, DH), F32), sds((1, 32, DH), F32), sds((32, DH), F32), sds((32, DH), F32),
    )
    args = [
        pltpu.with_memory_space_constraint(a, pltpu.HBM)
        for a in (q, rk, rv, tk, tv, hk, hv, g)]
    raw = pl.pallas_call(
        kernel,
        out_shape=shapes,
        in_specs=[smem, smem] + [hbm] * 8,
        out_specs=(vm,) * 7,
        scratch_shapes=[
            V((H * RESP, DH), BF16), V((H * RESP, DH), BF16),
            V((H, DH, RESP), BF16), V((H, DH, RESP), BF16),
            V((KEYS, DH), BF16), V((KEYS, DH), BF16), V((DH, KEYS), BF16),
            V((NP, 64, DH), BF16), V((NB, 64, DH), BF16),
            V((H, KEYS, RESP), F32), V((H, KEYS, RESP), F32), V((KEYS, H * RESP), BF16),
            V((H, 1, RESP), F32), V((H, 8, RESP), F32), V((H, 8, RESP), F32),
            V((NZ + 3, H, 1, RESP), F32), V((NZ + 3, H, 1, RESP), F32), V((H, 1, RESP), F32),
            V((NB, 64, DH), BF16), V((2 * NEAR_MAX + 1, SPOKES, 2, 64, DH), BF16),
            V((SPOKES, 2, 64, DH), BF16), V((SPOKES, 2, 64, DH), BF16),
            V((2 * NP, 32, DH), BF16), V((2 * NP, 32, DH), BF16),
            V((32, DH), BF16), V((NZ, 32, DH), BF16), V((2, 32, DH), BF16),
            dma((2 + 2 * H,)), dma((4,)),
            dma((48,)), dma((NP,)), dma((NB,)), dma((2,)),
            dma((NZ + 1,)), dma((2 * NEAR_MAX + 1, SPOKES)),
            dma((SPOKES, 2)), dma((SPOKES, 2)),
            dma((32,)), dma((32,)), dma((1,)), dma((NZ,)), dma((31,)), dma((2,)),
        ],
        compiler_params=pltpu.CompilerParams(
            collective_id=0, has_side_effects=True, vmem_limit_bytes=52 << 20),
    )(lengths, forks, *args)
    return pl.pallas_call(
        finish_kernel,
        out_shape=shapes,
        in_specs=(vm,) * 7,
        out_specs=(hbm,) * 7,
        scratch_shapes=[dma((7,))],
    )(*[pltpu.with_memory_space_constraint(a, pltpu.VMEM) for a in raw])


def solution(mesh):
    four, three, two = P("prompt", "branch", None, None), P("prompt", "branch", None), P("prompt", None)
    both = P("prompt", "branch")
    return jax.shard_map(
        per_device,
        mesh=mesh,
        in_specs=(four, four, four, three, three, two, two, four, both, both),
        out_specs=(four, four, four, three, three, two, two),
        check_vma=False,
    )
```

```python
import functools

import jax
import jax.numpy as jnp
from jax import lax
from jax.experimental import pallas as pl
from jax.experimental.pallas import tpu as pltpu
from jax.sharding import PartitionSpec as P

DH = 128
H = 8
BLK = 128
RESP = 256
HDR = 512
PREF = 1024
NP = 16
NB = 32
NZ = 16
CH = 256
KEYS = HDR + PREF + RESP
NCH = KEYS // CH
GATHER_STEP, GATHER_FARS = 3, 2
STEP, FARS = 5, 1
NEAR_MAX = STEP // 2
SPOKES = 2 * FARS + 1
REST = NZ // 2 - FARS * STEP
G_NEAR_MAX = GATHER_STEP // 2
G_REST = NZ // 2 - GATHER_FARS * GATHER_STEP
NEAR = tuple(j for j in range(-G_NEAR_MAX, G_NEAR_MAX + 1) if j != 0)
FAR = tuple(k * GATHER_STEP for k in range(-GATHER_FARS, GATHER_FARS + 1) if k != 0)
LOW = -1e30
SCALE = DH**-0.5
LOG2E = 1.4426950408889634
C2 = SCALE * LOG2E
UNROLL = 8
MESH = pl.DeviceIdType.MESH
F32 = jnp.float32
BF16 = jnp.bfloat16


def mod(a, n):
    return lax.rem(a + 4 * n, n)


def kernel(
    lengths, forks, q_hbm, rk_hbm, rv_hbm, tk_hbm, tv_hbm, hk_hbm, hv_hbm, g_hbm,
    dq_out, rkg_out, rvg_out, tkg_out, tvg_out, hkg_out, hvg_out,
    qf, gf, qt, gt, ka, va, kt, hkv, tkv, e_s, dp_s, ds_s, m_s, l_s, d_s, mb_s, fac_s, del_s, inv_s,
    tb, r1, cs, r2, hb, rh, zs, rz, rg,
    in_sem, own_sem, gs, hrs, trs, ars, s1, q1, s2, q2, sh, qh, sz, qz, sg, qg,
):
    p = lax.axis_index("prompt")
    b = lax.axis_index("branch")
    z = b // 2
    y = lax.rem(b, 2)
    yo = 1 - y
    plane = p * 2 + y

    def at(dz, yy):
        return mod(z + dz, NZ) * 2 + yy

    own = [
        pltpu.make_async_copy(hk_hbm, hkv.at[p, pl.ds(0, 32)], own_sem.at[0]),
        pltpu.make_async_copy(hv_hbm, hkv.at[p, pl.ds(32, 32)], own_sem.at[1]),
        pltpu.make_async_copy(tk_hbm.at[0], tkv.at[b, pl.ds(0, 32)], own_sem.at[2]),
        pltpu.make_async_copy(tv_hbm.at[0], tkv.at[b, pl.ds(32, 32)], own_sem.at[3]),
    ]
    for c in own:
        c.start()
    barrier = pltpu.get_barrier_semaphore()
    greet = [(p, at(k, y)) for k in FAR]
    greet += [(p, at(j, yy)) for j in sorted({*NEAR, -G_REST, G_REST}) for yy in (y, yo)]
    greet += [(p, at(0, yo))]
    greet += [(mod(p + o, NP), b) for o in range(1, NP)]
    for d in greet:
        pl.semaphore_signal(barrier, 1, device_id=d, device_id_type=MESH)

    loads = [
        pltpu.make_async_copy(rk_hbm.at[0, 0], ka.at[pl.ds(HDR + PREF, RESP)], in_sem.at[0]),
        pltpu.make_async_copy(rv_hbm.at[0, 0], va.at[pl.ds(HDR + PREF, RESP)], in_sem.at[1]),
    ]
    for h in range(H):
        loads.append(pltpu.make_async_copy(
            q_hbm.at[0, 0, :, pl.ds(h * DH, DH)], qf.at[pl.ds(h * RESP, RESP)], in_sem.at[2 + h]))
        loads.append(pltpu.make_async_copy(
            g_hbm.at[0, 0, :, pl.ds(h * DH, DH)], gf.at[pl.ds(h * RESP, RESP)], in_sem.at[2 + H + h]))
    for c in loads:
        c.start()

    for c in own:
        c.wait()
    pl.semaphore_wait(barrier, len(greet))

    sent = []

    def send(src, dst, ssem, rsem, dev):
        c = pltpu.make_async_remote_copy(
            src_ref=src, dst_ref=dst, send_sem=ssem, recv_sem=rsem, device_id=dev, device_id_type=MESH)
        c.start()
        sent.append(c)

    n = 0
    slots = [b] + [at(k, y) for k in FAR]
    for k in sorted(FAR, key=abs, reverse=True):
        send(tkv.at[b], tkv.at[b], gs.at[n], trs.at[b], (p, at(k, y)))
        n += 1
    near = [at(j, yy) for j in NEAR for yy in (y, yo)] + [at(0, yo)]
    for d in near:
        send(tkv.at[b], tkv.at[b], gs.at[n], trs.at[b], (p, d))
        n += 1
    for o in range(1, NP):
        send(hkv.at[p], hkv.at[p], gs.at[n], hrs.at[p], (mod(p + o, NP), b))
        n += 1

    for c in loads:
        c.wait()
    live = lax.broadcasted_iota(jnp.int32, (RESP, DH), 0) < lengths[0, 0]

    def prepare(h, _):
        rows = pl.ds(pl.multiple_of(h * RESP, RESP), RESP)
        g = jnp.where(live, gf[rows, :], jnp.zeros((), BF16))
        gf[rows, :] = g
        gt[h] = g.T
        qt[h] = qf[rows, :].T
        m_s[h] = jnp.full((1, RESP), LOW, F32)
        l_s[h] = jnp.zeros((8, RESP), F32)
        d_s[h] = jnp.zeros((8, RESP), F32)
        return 0

    lax.fori_loop(0, H, prepare, 0)
    r1[2 * NEAR_MAX, 0, :, :32, :] = jnp.zeros((2, 32, DH), BF16)
    for f in range(1, 2 * FARS):
        r1[2 * NEAR_MAX, f] = jnp.zeros((2, 64, DH), BF16)
    r1[2 * NEAR_MAX, 2 * FARS, :, 32:, :] = jnp.zeros((2, 32, DH), BF16)
    fork = forks[0, 0]

    def stats(h, spots, seen, kind):
        keys = [ka[pl.ds(r, c), :] for r, c in spots]
        vals = [va[pl.ds(r, c), :] for r, c in spots]
        keys = keys[0] if len(keys) == 1 else jnp.concatenate(keys, axis=0)
        vals = vals[0] if len(vals) == 1 else jnp.concatenate(vals, axis=0)
        s = jnp.dot(keys, qt[h], preferred_element_type=F32)
        dp = jnp.dot(vals, gt[h], preferred_element_type=F32)
        if kind == "resp":
            key = lax.broadcasted_iota(jnp.int32, s.shape, 0)
            pos = lax.broadcasted_iota(jnp.int32, s.shape, 1)
            s = jnp.where(key <= pos, s, LOW)
        m_old = m_s[h]
        m_new = m_old
        first = 0
        for (r, c), see in zip(spots, seen):
            top = jnp.max(s[first : first + c], axis=0, keepdims=True)
            m_new = jnp.maximum(m_new, top if see is None else jnp.where(see, top, LOW))
            first += c
        f = jnp.exp2((m_old - m_new) * C2)
        shift = m_new * C2
        l = l_s[h] * f
        d = d_s[h] * f
        first = 0
        for (r, c), see in zip(spots, seen):
            move = shift if see is None else jnp.where(see, shift, -LOW)
            e = jnp.exp2(s[first : first + c] * C2 - move)
            dpu = dp[first : first + c]
            l = l + jnp.sum(e.reshape(c // 8, 8, RESP), axis=0)
            d = d + jnp.sum((e * dpu).reshape(c // 8, 8, RESP), axis=0)
            e_s[h, pl.ds(r, c), :] = e
            dp_s[h, pl.ds(r, c), :] = dpu
            first += c
        l_s[h] = l
        d_s[h] = d
        m_s[h] = m_new
        return m_new

    def stats_of(spots, seen, kind, marks):
        def body(h, _):
            m = stats(h, spots, seen, kind)
            for k in marks:
                mb_s[k, h] = m
            return 0
        lax.fori_loop(0, H, body, 0, unroll=UNROLL)

    def trunk_stats(zs_here):
        for zb in zs_here:
            for w in range(2):
                r = pl.ds(pl.multiple_of(HDR + zb * 64 + w * 32, 32), 32)
                ka[r, :] = tkv[2 * zb + w, :32, :]
                va[r, :] = tkv[2 * zb + w, 32:, :]
        spots = [(pl.multiple_of(HDR + zb * 64, 64), 64) for zb in zs_here]
        seen = [jnp.broadcast_to(zb // 2, (1, RESP)) < fork for zb in zs_here]
        stats_of(spots, seen, "trunk", zs_here)

    stats_of([(HDR + PREF, RESP)], [None], "resp", [NZ + 2])

    def arrived(ref, sem):
        pltpu.make_async_remote_copy(
            src_ref=ref, dst_ref=ref, send_sem=gs.at[0], recv_sem=sem,
            device_id=(p, at(1, y)), device_id_type=MESH).wait_recv()

    kk, vv = pl.ds(0, 32), pl.ds(32, 32)
    def pass_on(k, n):
        s = at(k, y)
        arrived(tkv.at[s], trs.at[s])
        for d in near:
            send(tkv.at[s], tkv.at[s], gs.at[n], trs.at[s], (p, d))
            n += 1
        return n

    def group(k):
        for yy in (y, yo):
            for j in NEAR:
                arrived(tkv.at[at(k + j, yy)], trs.at[at(k + j, yy)])
        arrived(tkv.at[at(k, yo)], trs.at[at(k, yo)])
        return [mod(z + k + j, NZ) for j in (0, *NEAR)]

    by_distance = sorted(FAR, key=abs)
    for k in by_distance:
        if abs(k) == GATHER_STEP:
            n = pass_on(k, n)
    trunk_stats(group(0))
    for k in by_distance:
        if abs(k) > GATHER_STEP:
            n = pass_on(k, n)
    first, last = at(FAR[0], y), at(FAR[-1], y)
    for yy in (y, yo):
        send(tkv.at[first, kk], tkv.at[first, kk], gs.at[n], trs.at[first], (p, at(G_REST, yy)))
        n += 1
        send(tkv.at[last, vv], tkv.at[last, vv], gs.at[n], ars.at[y], (p, at(-G_REST, yy)))
        n += 1

    for o in range(1, NP):
        s = mod(p + o, NP)
        arrived(hkv.at[s], hrs.at[s])
    for i in range(NP):
        ka[pl.ds(i * 32, 32), :] = hkv[i, :32, :]
        va[pl.ds(i * 32, 32), :] = hkv[i, 32:, :]

    def head_stats(i, _):
        stats_of([(pl.multiple_of(i * CH, CH), CH)], [None], "head", [NZ + i])
        return 0

    lax.fori_loop(0, HDR // CH, head_stats, 0)

    def far_group(i, _):
        k = (i // 2 + 1) * GATHER_STEP * (1 - 2 * lax.rem(i, 2))
        trunk_stats(group(k))
        return 0

    lax.fori_loop(0, 2 * GATHER_FARS - 2, far_group, 0)
    last_group = group(GATHER_FARS * GATHER_STEP) + group(-GATHER_FARS * GATHER_STEP)
    anti = mod(z + 8, NZ)
    for yy in (y, yo):
        arrived(tkv.at[2 * anti + yy, kk], trs.at[2 * anti + yy])
        arrived(tkv.at[2 * anti + yy, vv], ars.at[yy])
    trunk_stats(last_group + [anti])

    def finish(h, _):
        inv = 1.0 / jnp.sum(l_s[h], axis=0, keepdims=True)
        del_s[h] = jnp.sum(d_s[h], axis=0, keepdims=True) * inv
        m = m_s[h]
        inv_s[h] = inv
        for i in range(NZ, NZ + 3):
            fac_s[i, h] = jnp.exp2((mb_s[i, h] - m) * C2) * inv
        return 0

    lax.fori_loop(0, H, finish, 0, unroll=UNROLL)

    def finish_trunk(h, _):
        for i in range(NZ):
            fac_s[i, h] = jnp.exp2((mb_s[i, h] - m_s[h]) * C2) * inv_s[h]
        return 0

    def terms(first, marks):
        rows = pl.ds(first, CH)
        c = CH // len(marks)
        kg = jnp.zeros((CH, DH), F32)
        vg = jnp.zeros((CH, DH), F32)
        for h in range(H):
            pr = [e_s[h, pl.ds(first + u * c, c), :] * fac_s[k, h] for u, k in enumerate(marks)]
            pr = pr[0] if len(pr) == 1 else jnp.concatenate(pr, axis=0)
            ds = (pr * (dp_s[h, rows, :] - del_s[h])).astype(BF16)
            ds_s[rows, h * RESP : (h + 1) * RESP] = ds
            kg = kg + jnp.dot(ds, qf[h * RESP : (h + 1) * RESP, :], preferred_element_type=F32)
            vg = vg + jnp.dot(pr.astype(BF16), gf[h * RESP : (h + 1) * RESP, :], preferred_element_type=F32)
        return kg * SCALE, vg

    def head_copy(q):
        return pltpu.make_async_remote_copy(
            src_ref=hb.at[q], dst_ref=rh.at[plane], send_sem=sh.at[q], recv_sem=qh.at[plane],
            device_id=(q // 2, z * 2 + lax.rem(q, 2)), device_id_type=MESH)

    def head_terms(i, _):
        kg, vg = terms(pl.multiple_of(i * CH, CH), [NZ + i])
        kg, vg = kg.astype(BF16), vg.astype(BF16)
        for u in range(CH // 16):
            hb[i * (CH // 16) + u, :16, :] = kg[u * 16 : (u + 1) * 16]
            hb[i * (CH // 16) + u, 16:, :] = vg[u * 16 : (u + 1) * 16]
        return 0

    lax.fori_loop(0, HDR // CH, head_terms, 0)
    for o in range(1, 2 * NP):
        head_copy(mod(plane + o, 2 * NP)).start()

    def route(zd):
        o = mod(zd - z, NZ)
        signed = jnp.where(o > NZ // 2, o - NZ, o)
        f = (signed + NEAR_MAX + FARS * STEP) // STEP
        j = signed - (f - FARS) * STEP
        jn = jnp.where(j < 0, j + NEAR_MAX, j + NEAR_MAX - 1)
        ok = jnp.logical_and(o != NZ // 2, j != 0)
        return o, ok, jnp.where(ok, j, 1), jnp.where(ok, jn, 0), jnp.where(ok, f, 0)

    def near_copies(zd):
        o, ok, j, jn, f = route(zd)
        whole = pltpu.make_async_remote_copy(
            src_ref=tb.at[pl.ds(2 * zd, 2)], dst_ref=r1.at[jn, f], send_sem=s1.at[zd], recv_sem=q1.at[jn, f],
            device_id=(p, mod(z + j, NZ) * 2 + y), device_id_type=MESH)
        low = pltpu.make_async_remote_copy(
            src_ref=tb.at[pl.ds(2 * zd, 2), kk], dst_ref=r1.at[2 * NEAR_MAX, 2 * FARS, :, kk],
            send_sem=s1.at[zd], recv_sem=q1.at[2 * NEAR_MAX, 2 * FARS],
            device_id=(p, at(REST, y)), device_id_type=MESH)
        high = pltpu.make_async_remote_copy(
            src_ref=tb.at[pl.ds(2 * zd, 2), vv], dst_ref=r1.at[2 * NEAR_MAX, 0, :, vv],
            send_sem=s1.at[NZ], recv_sem=q1.at[2 * NEAR_MAX, 0],
            device_id=(p, at(-REST, y)), device_id_type=MESH)
        return ok, o == NZ // 2, whole, low, high

    def trunk_terms(i, _):
        kg, vg = terms(pl.multiple_of(HDR + i * CH, CH), [i * 4 + u for u in range(4)])
        kg, vg = kg.astype(BF16), vg.astype(BF16)
        for u in range(CH // 32):
            k = i * (CH // 32) + u
            tb[k, :32, :] = kg[u * 32 : (u + 1) * 32]
            tb[k, 32:, :] = vg[u * 32 : (u + 1) * 32]
        for u in range(4):
            one, two, whole, low, high = near_copies(i * 4 + u)

            @pl.when(one)
            def _():
                whole.start()

            @pl.when(two)
            def _():
                low.start()
                high.start()
        return 0

    lax.fori_loop(0, H, finish_trunk, 0, unroll=UNROLL)
    lax.fori_loop(0, PREF // CH, trunk_terms, 0)

    acc = hb[plane].astype(F32)
    for o in range(1, 2 * NP):
        s = mod(plane + o, 2 * NP)
        arrived(rh.at[s], qh.at[s])
        acc = acc + rh[s].astype(F32)
    zs[...] = acc.astype(BF16)

    @pl.when(z != 0)
    def _():
        pltpu.make_async_remote_copy(
            src_ref=zs, dst_ref=rz.at[z], send_sem=sz.at[0], recv_sem=qz.at[z],
            device_id=(p, y), device_id_type=MESH).start()

    kg, vg = terms(HDR + PREF, [NZ + 2])
    rkg_out[0, 0] = kg.astype(BF16)
    rvg_out[0, 0] = vg.astype(BF16)

    kt[...] = ka[...].T

    def query_grad(h, _):
        cols = pl.ds(pl.multiple_of(h * RESP, RESP), RESP)
        acc = jnp.dot(kt[...], ds_s[:, cols], preferred_element_type=F32)
        dq_out[0, 0, :, pl.ds(pl.multiple_of(h * DH, DH), DH)] = (acc * SCALE).T.astype(BF16)
        return 0

    lax.fori_loop(0, H // 2, query_grad, 0)

    dests = [mod(z + (f - FARS) * STEP, NZ) for f in range(SPOKES)]
    ranks = [sum((other < d).astype(jnp.int32) for other in dests) for d in dests]
    for k in range(SPOKES):
        f = sum(jnp.where(r == k, i, 0) for i, r in enumerate(ranks))
        zd = mod(z + (f - FARS) * STEP, NZ)
        for jn in range(2 * NEAR_MAX):
            arrived(r1.at[jn, f], q1.at[jn, f])

        @pl.when(f == 0)
        def _():
            arrived(r1.at[2 * NEAR_MAX, 0, :, vv], q1.at[2 * NEAR_MAX, 0])

        @pl.when(f == 2 * FARS)
        def _():
            arrived(r1.at[2 * NEAR_MAX, 2 * FARS, :, kk], q1.at[2 * NEAR_MAX, 2 * FARS])

        total = tb[pl.ds(2 * zd, 2)].astype(F32)
        for jn in range(2 * NEAR_MAX + 1):
            total = total + r1[jn, f].astype(F32)
        cs[f] = total.astype(BF16)

        @pl.when(f != FARS)
        def _():
            pltpu.make_async_remote_copy(
                src_ref=cs.at[f, y], dst_ref=r2.at[f, 0], send_sem=s2.at[f, 0], recv_sem=q2.at[f, 0],
                device_id=(p, zd * 2 + y), device_id_type=MESH).start()

        pltpu.make_async_remote_copy(
            src_ref=cs.at[f, yo], dst_ref=r2.at[f, 1], send_sem=s2.at[f, 1], recv_sem=q2.at[f, 1],
            device_id=(p, zd * 2 + yo), device_id_type=MESH).start()

    def head_copies():
        out = []
        for dz in (0, 1, -1, 2, -2, 3, -3, 4, -4, 5, -5, 6, -6, 7, -7, 8):
            for w, yy in enumerate((y, yo)):
                if dz == 0 and w == 0:
                    continue
                out.append(pltpu.make_async_remote_copy(
                    src_ref=rg.at[y], dst_ref=rg.at[y], send_sem=sg.at[len(out)], recv_sem=qg.at[y],
                    device_id=(p, at(dz, yy)), device_id_type=MESH))
        return out

    lax.fori_loop(H // 2, H, query_grad, 0)

    @pl.when(z == 0)
    def _():
        total = acc
        for i in sorted(range(1, NZ), key=lambda i: min(i, NZ - i)):
            arrived(rz.at[i], qz.at[i])
            total = total + rz[i].astype(F32)
        rg[y] = total.astype(BF16)
        for i, c in enumerate(head_copies()):
            c.start()

    for c in sent:
        c.wait_send()
    for zd in range(NZ):
        one, two, whole, low, high = near_copies(zd)

        @pl.when(one)
        def _():
            whole.wait_send()

        @pl.when(two)
        def _():
            low.wait_send()
            high.wait_send()

    for q in range(2 * NP):

        @pl.when(q != plane)
        def _():
            head_copy(q).wait_send()

    spokes = [(f, w) for f in range(SPOKES) for w in range(2) if (f, w) != (FARS, 0)]
    for f, w in spokes:
        arrived(r2.at[f, w], q2.at[f, w])
    total = cs[FARS, y].astype(F32)
    for f, w in spokes:
        total = total + r2[f, w].astype(F32)
    tkg_out[0] = total[:32]
    tvg_out[0] = total[32:]

    arrived(rg.at[yo], qg.at[yo])

    @pl.when(z != 0)
    def _():
        arrived(rg.at[y], qg.at[y])

    for w in range(2):
        hkg_out[w * 16 : (w + 1) * 16, :] = rg[w, :16, :].astype(F32)
        hvg_out[w * 16 : (w + 1) * 16, :] = rg[w, 16:, :].astype(F32)

    for f, w in spokes:
        pltpu.make_async_remote_copy(
            src_ref=cs.at[f, w], dst_ref=r2.at[f, w], send_sem=s2.at[f, w], recv_sem=q2.at[f, w],
            device_id=(p, at(1, y)), device_id_type=MESH).wait_send()
    @pl.when(z != 0)
    def _():
        pltpu.make_async_remote_copy(
            src_ref=zs, dst_ref=rz.at[z], send_sem=sz.at[0], recv_sem=qz.at[z],
            device_id=(p, y), device_id_type=MESH).wait_send()

    @pl.when(z == 0)
    def _():
        for c in head_copies():
            c.wait_send()


def finish_kernel(*refs):
    ins, outs, sem = refs[:7], refs[7:14], refs[14]
    copies = [pltpu.make_async_copy(a, o, sem.at[i]) for i, (a, o) in enumerate(zip(ins, outs))]
    for c in copies:
        c.start()
    for c in copies:
        c.wait()


def per_device(q, rk, rv, tk, tv, hk, hv, g, lengths, forks):
    vm = pl.BlockSpec(memory_space=pltpu.VMEM)
    hbm = pl.BlockSpec(memory_space=pltpu.HBM)
    smem = pl.BlockSpec(memory_space=pltpu.SMEM)
    dma = pltpu.SemaphoreType.DMA
    sds = jax.ShapeDtypeStruct
    V = pltpu.VMEM
    shapes = (
            sds((1, 1, RESP, H * DH), BF16), sds((1, 1, RESP, DH), BF16), sds((1, 1, RESP, DH), BF16),
            sds((1, 32, DH), F32), sds((1, 32, DH), F32), sds((32, DH), F32), sds((32, DH), F32),
    )
    args = [
        pltpu.with_memory_space_constraint(a, pltpu.HBM)
        for a in (q, rk, rv, tk, tv, hk, hv, g)]
    raw = pl.pallas_call(
        kernel,
        out_shape=shapes,
        in_specs=[smem, smem] + [hbm] * 8,
        out_specs=(vm,) * 7,
        scratch_shapes=[
            V((H * RESP, DH), BF16), V((H * RESP, DH), BF16),
            V((H, DH, RESP), BF16), V((H, DH, RESP), BF16),
            V((KEYS, DH), BF16), V((KEYS, DH), BF16), V((DH, KEYS), BF16),
            V((NP, 64, DH), BF16), V((NB, 64, DH), BF16),
            V((H, KEYS, RESP), F32), V((H, KEYS, RESP), F32), V((KEYS, H * RESP), BF16),
            V((H, 1, RESP), F32), V((H, 8, RESP), F32), V((H, 8, RESP), F32),
            V((NZ + 3, H, 1, RESP), F32), V((NZ + 3, H, 1, RESP), F32), V((H, 1, RESP), F32), V((H, 1, RESP), F32),
            V((NB, 64, DH), BF16), V((2 * NEAR_MAX + 1, SPOKES, 2, 64, DH), BF16),
            V((SPOKES, 2, 64, DH), BF16), V((SPOKES, 2, 64, DH), BF16),
            V((2 * NP, 32, DH), BF16), V((2 * NP, 32, DH), BF16),
            V((32, DH), BF16), V((NZ, 32, DH), BF16), V((2, 32, DH), BF16),
            dma((2 + 2 * H,)), dma((4,)),
            dma((48,)), dma((NP,)), dma((NB,)), dma((2,)),
            dma((NZ + 1,)), dma((2 * NEAR_MAX + 1, SPOKES)),
            dma((SPOKES, 2)), dma((SPOKES, 2)),
            dma((32,)), dma((32,)), dma((1,)), dma((NZ,)), dma((31,)), dma((2,)),
        ],
        compiler_params=pltpu.CompilerParams(
            collective_id=0, has_side_effects=True, vmem_limit_bytes=52 << 20),
    )(lengths, forks, *args)
    return pl.pallas_call(
        finish_kernel,
        out_shape=shapes,
        in_specs=(vm,) * 7,
        out_specs=(hbm,) * 7,
        scratch_shapes=[dma((7,))],
    )(*[pltpu.with_memory_space_constraint(a, pltpu.VMEM) for a in raw])


def solution(mesh):
    four, three, two = P("prompt", "branch", None, None), P("prompt", "branch", None), P("prompt", None)
    both = P("prompt", "branch")
    return jax.shard_map(
        per_device,
        mesh=mesh,
        in_specs=(four, four, four, three, three, two, two, four, both, both),
        out_specs=(four, four, four, three, three, two, two),
        check_vma=False,
    )
```
